512 devices in a mesh: row: 16 (over z, x_lo), col: 32 (over y, x_hi, core).
Axes of the slice: x: 4 (x_hi: 2, x_lo: 2; x = x_hi * 2 + x_lo), y: 8, z: 8, core: 2. Of those that a mesh axis runs over, the one named last changes fastest.
Arguments:
- points: float32 [64, 65536], P(None, ('row', 'col')), may hold values from -6 to 6
- inv_scale: float32 [64], replicated, may hold values from 0.2 to 0.6
- noise_var: float32 [65536], P(('row', 'col')), may hold values from 1 to 16
- residual: float32 [16, 65536], P(None, ('row', 'col')), may hold values from -45 to 45
- direction: float32 [16, 65536], P(None, ('row', 'col')), may hold values from -45 to 45
Outputs:
- residual_next: float32 [16, 65536], P(None, ('row', 'col'))
- direction_next: float32 [16, 65536], P(None, ('row', 'col'))
The draws below stay inside these ranges and needn't reach their ends.
All inputs are finite; a program needn't handle non-finite values.
Results may differ from the reference program's by a relative error of at most 0.0021.
Values may be sent and summed in bfloat16 or wider, within the bound.
A program may use at most 128 MiB of HBM per device.

```python
import math
import jax
import jax.numpy as jnp
from jax import lax

F = 64
R = 16
POINTS = 65536


def scaled_field(key, base):
    pt_key, col_key = jax.random.split(key, 2)
    position = jnp.arange(POINTS, dtype=jnp.float32) / POINTS
    point_scale = jnp.exp(jnp.log(3.0) * position + jax.random.uniform(pt_key, (POINTS,), jnp.float32) * jnp.log(3.3))
    column_scale = jnp.exp(jax.random.uniform(col_key, (R, 1), jnp.float32) * jnp.log(10.0))
    return 0.1 * base * column_scale * point_scale[None, :]


def draw_points(key, part):
    key = jax.random.fold_in(key, 7)
    latent_key, gain_key, spread_key = jax.random.split(key, 3)
    latent_count = min(10, F)
    latent = jax.random.truncated_normal(latent_key, -4.0, 4.0, (latent_count, POINTS), jnp.float32)
    feature_gain = jax.random.uniform(gain_key, (F, 1), jnp.float32, 0.8, 1.2)
    spread = jax.random.truncated_normal(spread_key, -4.0, 4.0, (F, POINTS), jnp.float32)
    picked = latent[jnp.arange(F, dtype=jnp.int32) % latent_count]
    return picked * feature_gain + 0.2 * spread


def draw_residual(key, part):
    key = jax.random.fold_in(key, 11)
    base_key, rest_key = jax.random.split(key, 2)
    base = jax.random.truncated_normal(base_key, -4.0, 4.0, (R, POINTS), jnp.float32)
    return scaled_field(rest_key, base)


def draw_direction(key, part):
    key = jax.random.fold_in(key, 23)
    base_key, rest_key = jax.random.split(key, 2)
    base = jax.random.truncated_normal(base_key, -4.0, 4.0, (R, POINTS), jnp.float32)
    return scaled_field(rest_key, base)


def block_scale(stream_key, shape, cuts, low, largest):
    level, own = 1.0, jax.random.fold_in(stream_key, 6)
    for dim, parts in cuts:
        steps = jnp.exp(jax.random.uniform(jax.random.fold_in(own, dim), (parts,), jnp.float32, low / len(cuts), largest / len(cuts)))
        level = level * jnp.repeat(steps, shape[dim] // parts).reshape([-1 if axis == dim else 1 for axis in range(len(shape))])
    return level


def setup_inputs(seed: int = 0) -> dict:
    arg_keys = jax.random.split(jax.random.key(seed), 6)
    points = draw_points(jax.random.fold_in(arg_keys[5], 71), 0)
    inv_scale = jnp.clip(jnp.exp(jax.random.uniform(arg_keys[1], (F,), jnp.float32, math.log(0.2), math.log(0.6))), 0.2, 0.6)
    noise_var = jnp.clip(jnp.exp(math.log(16.0) - 2.7725887 * jax.random.uniform(arg_keys[2], (POINTS,), jnp.float32) ** block_scale(arg_keys[2], (POINTS,), ((0, 512),), -0.2, 0.2)), 1.0, 16.0)
    residual = draw_residual(jax.random.fold_in(arg_keys[5], 71), 0)
    direction = draw_direction(jax.random.fold_in(arg_keys[5], 71), 0)
    return {"points": points, "inv_scale": inv_scale, "noise_var": noise_var, "residual": residual, "direction": direction}


def reference(points, inv_scale, noise_var, residual, direction):
    scaled = points * inv_scale[:, None]
    sq_norms = jnp.sum(scaled * scaled, axis=0)
    low_dirs = direction.astype(jnp.bfloat16)
    block_size = math.gcd(POINTS, 512)

    def block_product(block_index):
        offset = block_index.astype(jnp.int32) * block_size
        row_points = lax.dynamic_slice_in_dim(scaled, offset, block_size, 1)
        row_norms = lax.dynamic_slice_in_dim(sq_norms, offset, block_size, 0)
        cross_terms = lax.dot_general(row_points, scaled, (((0,), (0,)), ((), ())),
                                      precision=lax.Precision.HIGHEST,
                                      preferred_element_type=jnp.float32)
        kernel = jnp.exp(-0.5 * (row_norms[:, None] + sq_norms[None, :] - 2.0 * cross_terms)).astype(jnp.bfloat16)
        return lax.dot_general(low_dirs, kernel, (((1,), (1,)), ((), ())),
                               preferred_element_type=jnp.float32)

    blocks = lax.map(block_product, jnp.arange(POINTS // block_size, dtype=jnp.int32))
    kernel_image = jnp.transpose(blocks, (1, 0, 2)).reshape(R, POINTS) + noise_var[None, :] * direction
    norms_now = jnp.sum(residual * residual, axis=1)
    curvature = jnp.sum(direction * kernel_image, axis=1)
    step_size = norms_now / curvature
    residual_next = residual - step_size[:, None] * kernel_image
    norms_next = jnp.sum(residual_next * residual_next, axis=1)
    direction_next = residual_next + (norms_next / norms_now)[:, None] * direction
    return residual_next, direction_next
```

```python
import functools
import math

import jax
import jax.numpy as jnp
from jax import lax
from jax.experimental import pallas as pl
from jax.experimental.pallas import tpu as pltpu
from jax.sharding import PartitionSpec as P

MESH = pl.DeviceIdType.MESH
F = 64
R = 16
B = 128
ROWS, COLS = 16, 32
HALF = COLS // 2
MSG = F + R
DEPTH = 256
KEEP = 48
CODE = 250.0 / 6.0
BIAS = 125.0
SQRT_LOG2E = math.sqrt(math.log2(math.e))
bf16, f32 = jnp.bfloat16, jnp.float32


def encode(x):
    mag = jnp.exp2(jnp.abs(x) * CODE - BIAS)
    return jnp.where(x < 0, -mag, mag).astype(bf16)


def decode(code, factor):
    y = code.astype(f32)
    mag = (jnp.log2(jnp.abs(y)) + BIAS) * factor
    return jnp.where(y < 0, -mag, mag)


def split(a):
    hi = a.astype(bf16)
    hi32 = hi.astype(f32)
    mid = (a - hi32).astype(bf16)
    mid32 = mid.astype(f32)
    norm = -jnp.sum(hi32 * (0.5 * hi32 + mid32), axis=0, keepdims=True)
    n0 = norm.astype(bf16).astype(f32)
    n1 = (norm - n0).astype(bf16).astype(f32)
    n2 = norm - n0 - n1
    return hi, mid, (n0, n1, n2)


def aux_rows(norms, first):
    row = lax.broadcasted_iota(jnp.int32, (16, B), 0)
    out = jnp.where((row >= 3 - first) & (row < 6 - first), 1.0, 0.0)
    for i, n in enumerate(norms):
        out = jnp.where(row == first + i, n, out)
    return out.astype(bf16)


def j_operand(a):
    hi, mid, norms = split(a)
    return jnp.concatenate([hi, mid, hi, mid[:KEEP], aux_rows(norms, 3)], axis=0)


def i_operand(a):
    hi, mid, norms = split(a)
    return jnp.concatenate([hi, hi, mid, mid[:KEEP], aux_rows(norms, 0)], axis=0).T


def kernel(
    points, scale, noise, residual, direction, res_out, dir_out,
    send, jbuf, ibuf, jop, jdir, jacc, obuf, cpart, rpart, sums, csum, sums2, rsum,
    send_sem, jsem, isem, osend, csem, rsem, ssend, ssem, ssem2,
):
    r, c = lax.axis_index("row"), lax.axis_index("col")

    def row_peer(d):
        return (lax.rem(r + d, ROWS), c)

    def col_peer(d):
        return (r, lax.rem(c + d + COLS, COLS))

    def shift(i):
        return jnp.where(lax.rem(i, 2) == 1, i, -i)

    barrier = pltpu.get_barrier_semaphore()

    def greet_row(d, _):
        pl.semaphore_signal(barrier, inc=1, device_id=row_peer(d), device_id_type=MESH)
        return _

    def greet_col(i, _):
        pl.semaphore_signal(barrier, inc=1, device_id=col_peer(shift(i)), device_id_type=MESH)
        return _

    lax.fori_loop(1, ROWS, greet_row, 0)
    lax.fori_loop(1, HALF + 1, greet_col, 0)

    dirs = direction[...]
    send[:F, :] = encode(points[...])
    send[F:, :] = dirs.astype(bf16)
    factor = jnp.broadcast_to(scale[...], (B, F)).T * (SQRT_LOG2E / CODE)

    pl.semaphore_wait(barrier, ROWS - 1 + HALF)

    def to_row(d):
        return pltpu.make_async_remote_copy(
            src_ref=send, dst_ref=jbuf.at[d - 1], send_sem=send_sem, recv_sem=jsem.at[d - 1],
            device_id=row_peer(ROWS - d), device_id_type=MESH)

    def to_col(i):
        return pltpu.make_async_remote_copy(
            src_ref=send, dst_ref=ibuf.at[i - 1], send_sem=send_sem, recv_sem=isem.at[i - 1],
            device_id=col_peer(-shift(i)), device_id_type=MESH)

    def push(k, _):
        @pl.when(k < ROWS)
        def _row():
            to_row(k).start()
        to_col(k).start()
        return _

    lax.fori_loop(1, HALF + 1, push, 0)

    def put_j(d, msg):
        jop[d] = j_operand(decode(msg[:F], factor))
        jdir[d] = msg[F:]
        jacc[d] = jnp.zeros((R, B), f32)

    put_j(0, send[...])

    def take_j(k, _):
        d = jnp.where(lax.rem(k, 2) == 1, lax.div(k + 1, 2), ROWS - lax.div(k, 2))
        to_row(d).wait_recv()
        put_j(d, jbuf[d - 1])
        return _

    lax.fori_loop(1, ROWS, take_j, 0)

    def tile(left, idir, d, both):
        s = jnp.dot(left, jop[d], preferred_element_type=f32)
        p = jnp.exp2(s).astype(bf16)
        if both:
            jacc[d] += jnp.dot(idir, p, preferred_element_type=f32)
        return lax.dot_general(jdir[d], p, (((1,), (1,)), ((), ())), preferred_element_type=f32)

    def i_block(i, msg, one_way, both_ways):
        left = i_operand(decode(msg[:F], factor))
        idir = msg[F:]
        acc = jnp.zeros((R, B), f32)
        for d in range(ROWS):
            if d in one_way or d in both_ways:
                acc += tile(left, idir, d, d in both_ways)
        obuf[i] = acc

    def to_owner(i):
        return pltpu.make_async_remote_copy(
            src_ref=obuf.at[i], dst_ref=cpart.at[i - 1], send_sem=osend, recv_sem=csem,
            device_id=col_peer(shift(i)), device_id_type=MESH)

    half = dict(one_way=(0, ROWS // 2), both_ways=range(1, ROWS // 2))
    i_block(0, send[...], **half)

    def take_i(i, _):
        to_col(i).wait_recv()
        i_block(i, ibuf[i - 1], (), range(ROWS))
        to_owner(i).start()
        return _

    lax.fori_loop(1, HALF, take_i, 0)
    to_col(HALF).wait_recv()
    i_block(HALF, ibuf[HALF - 1], **half)
    to_owner(HALF).start()

    def to_row_owner(d):
        return pltpu.make_async_remote_copy(
            src_ref=jacc.at[d], dst_ref=rpart.at[d - 1], send_sem=osend, recv_sem=rsem,
            device_id=row_peer(d), device_id_type=MESH)

    def push_j(d, _):
        to_row_owner(d).start()
        return _

    lax.fori_loop(1, ROWS, push_j, 0)

    res = residual[...]
    total = obuf[0] + jacc[0] + noise[...] * dirs

    def whole(src, dst, s_sem, r_sem):
        return pltpu.make_async_remote_copy(
            src_ref=src, dst_ref=dst, send_sem=s_sem, recv_sem=r_sem,
            device_id=row_peer(1), device_id_type=MESH)

    whole(cpart, cpart, osend, csem).wait_recv()
    total += jnp.sum(cpart[...], axis=0)
    whole(rpart, rpart, osend, rsem).wait_recv()
    image = total + jnp.sum(rpart[...], axis=0)

    lane = lax.broadcasted_iota(jnp.int32, (R, B), 1)
    local = jnp.zeros((R, B), f32)
    for n, prod in enumerate((res * res, res * image, dirs * image, image * image)):
        local = jnp.where(lane == n, jnp.sum(prod, axis=1, keepdims=True), local)
    sums[...] = local

    def sum_to_col(d):
        return pltpu.make_async_remote_copy(
            src_ref=sums, dst_ref=csum.at[d - 1], send_sem=ssend, recv_sem=ssem,
            device_id=col_peer(d), device_id_type=MESH)

    def push_c(d, _):
        sum_to_col(d).start()
        return _

    lax.fori_loop(1, COLS, push_c, 0)
    whole(csum, csum, ssend, ssem).wait_recv()
    sums2[...] = sums[...] + jnp.sum(csum[...], axis=0)

    def sum_to_row(d):
        return pltpu.make_async_remote_copy(
            src_ref=sums2, dst_ref=rsum.at[d - 1], send_sem=ssend, recv_sem=ssem2,
            device_id=row_peer(d), device_id_type=MESH)

    def push_r(d, _):
        sum_to_row(d).start()
        return _

    lax.fori_loop(1, ROWS, push_r, 0)
    whole(rsum, rsum, ssend, ssem2).wait_recv()
    tot = sums2[...] + jnp.sum(rsum[...], axis=0)
    rr, rq, dq, qq = tot[:, 0:1], tot[:, 1:2], tot[:, 2:3], tot[:, 3:4]
    step = rr / dq
    nxt = rr - 2.0 * step * rq + step * (step * qq)
    res_next = res - step * image
    res_out[...] = res_next
    dir_out[...] = res_next + (nxt / rr) * dirs

    whole(jbuf, jbuf, send_sem, jsem.at[0]).wait_send()
    whole(ibuf, ibuf, send_sem, jsem.at[0]).wait_send()
    whole(cpart, cpart, osend, csem).wait_send()
    whole(rpart, rpart, osend, rsem).wait_send()
    whole(csum, csum, ssend, ssem).wait_send()
    whole(rsum, rsum, ssend, ssem2).wait_send()


def on_device(points, inv_scale, noise_var, residual, direction):
    vmem = pl.BlockSpec(memory_space=pltpu.VMEM)
    dma = pltpu.SemaphoreType.DMA
    out = jax.ShapeDtypeStruct((R, B), f32)
    return pl.pallas_call(
        kernel,
        out_shape=(out, out),
        in_specs=[vmem] * 5,
        out_specs=(vmem, vmem),
        scratch_shapes=[
            pltpu.VMEM((MSG, B), bf16),
            pltpu.VMEM((ROWS - 1, MSG, B), bf16),
            pltpu.VMEM((HALF, MSG, B), bf16),
            pltpu.VMEM((ROWS, DEPTH, B), bf16),
            pltpu.VMEM((ROWS, R, B), bf16),
            pltpu.VMEM((ROWS, R, B), f32),
            pltpu.VMEM((HALF + 1, R, B), f32),
            pltpu.VMEM((HALF, R, B), f32),
            pltpu.VMEM((ROWS - 1, R, B), f32),
            pltpu.VMEM((R, B), f32),
            pltpu.VMEM((COLS - 1, R, B), f32),
            pltpu.VMEM((R, B), f32),
            pltpu.VMEM((ROWS - 1, R, B), f32),
            dma, dma((ROWS - 1,)), dma((HALF,)), dma, dma, dma, dma, dma, dma,
        ],
        compiler_params=pltpu.CompilerParams(
            collective_id=0, has_side_effects=True, vmem_limit_bytes=32 << 20),
    )(points, inv_scale.reshape(1, F), noise_var.reshape(1, B), residual, direction)


def solution(mesh):
    split_points = P(None, ("row", "col"))
    return jax.shard_map(
        on_device,
        mesh=mesh,
        in_specs=(split_points, P(), P(("row", "col")), split_points, split_points),
        out_specs=(split_points, split_points),
        check_vma=False,
    )
```

```python
import functools
import math

import jax
import jax.numpy as jnp
from jax import lax
from jax.experimental import pallas as pl
from jax.experimental.pallas import tpu as pltpu
from jax.sharding import PartitionSpec as P

MESH = pl.DeviceIdType.MESH
F = 64
R = 16
B = 128
ROWS, COLS = 16, 32
HALF = COLS // 2
MSG = F + R
DEPTH = 256
KEEP = 48
CHUNK = 512
CODE = 250.0 / 6.0
BIAS = 125.0
SQRT_LOG2E = math.sqrt(math.log2(math.e))
bf16, f32 = jnp.bfloat16, jnp.float32


def encode(x):
    mag = jnp.exp2(jnp.abs(x) * CODE - BIAS)
    return jnp.where(x < 0, -mag, mag).astype(bf16)


def decode(code, factor):
    y = code.astype(f32)
    mag = (jnp.log2(jnp.abs(y)) + BIAS) * factor
    return jnp.where(y < 0, -mag, mag)


def split(a):
    hi = a.astype(bf16)
    hi32 = hi.astype(f32)
    mid = (a - hi32).astype(bf16)
    mid32 = mid.astype(f32)
    norm = -jnp.sum(hi32 * (0.5 * hi32 + mid32), axis=0, keepdims=True)
    n0 = norm.astype(bf16).astype(f32)
    n1 = (norm - n0).astype(bf16).astype(f32)
    n2 = norm - n0 - n1
    return hi, mid, (n0, n1, n2)


def aux_rows(norms, first):
    row = lax.broadcasted_iota(jnp.int32, (16, norms[0].shape[1]), 0)
    out = jnp.where((row >= 3 - first) & (row < 6 - first), 1.0, 0.0)
    for i, n in enumerate(norms):
        out = jnp.where(row == first + i, n, out)
    return out.astype(bf16)


def j_operand(a):
    hi, mid, norms = split(a)
    return jnp.concatenate([hi, mid, hi, mid[:KEEP], aux_rows(norms, 3)], axis=0)


def i_operand(a):
    hi, mid, norms = split(a)
    return jnp.concatenate([hi, hi, mid, mid[:KEEP], aux_rows(norms, 0)], axis=0).T


def kernel(
    points, scale, noise, residual, direction, res_out, dir_out,
    send, jbuf, ibuf, jop, jdir, jacc, probs, obuf, cpart, rpart, sums, csum, sums2, rsum,
    send_sem, jsem, isem, osend, csem, rsem, ssend, ssem, ssem2,
):
    r, c = lax.axis_index("row"), lax.axis_index("col")

    def row_peer(d):
        return (lax.rem(r + d, ROWS), c)

    def col_peer(d):
        return (r, lax.rem(c + d + COLS, COLS))

    def shift(i):
        return jnp.where(lax.rem(i, 2) == 1, i, -i)

    barrier = pltpu.get_barrier_semaphore()

    def greet_row(d, _):
        pl.semaphore_signal(barrier, inc=1, device_id=row_peer(d), device_id_type=MESH)
        return _

    def greet_col(i, _):
        pl.semaphore_signal(barrier, inc=1, device_id=col_peer(shift(i)), device_id_type=MESH)
        return _

    lax.fori_loop(1, ROWS, greet_row, 0)
    lax.fori_loop(1, HALF + 1, greet_col, 0)

    dirs = direction[...]
    send[:F, :] = encode(points[...])
    send[F:, :] = dirs.astype(bf16)
    factor = jnp.broadcast_to(scale[...], (B, F)).T[:, :1] * (SQRT_LOG2E / CODE)

    pl.semaphore_wait(barrier, ROWS - 1 + HALF)

    def to_row(d):
        return pltpu.make_async_remote_copy(
            src_ref=send, dst_ref=jbuf.at[d - 1], send_sem=send_sem, recv_sem=jsem.at[d - 1],
            device_id=row_peer(ROWS - d), device_id_type=MESH)

    def to_col(i):
        return pltpu.make_async_remote_copy(
            src_ref=send, dst_ref=ibuf.at[i - 1], send_sem=send_sem, recv_sem=isem.at[i - 1],
            device_id=col_peer(-shift(i)), device_id_type=MESH)

    def push(k, _):
        @pl.when(k < ROWS)
        def _row():
            to_row(k).start()
        to_col(k).start()
        return _

    lax.fori_loop(1, HALF + 1, push, 0)

    def slot(d):
        return pl.ds(pl.multiple_of(d * B, B), B)

    def put_j(d, msg):
        jop[:, slot(d)] = j_operand(decode(msg[:F], factor))
        jdir[:, slot(d)] = msg[F:]

    put_j(0, send[...])

    def take_j(k, _):
        d = jnp.where(lax.rem(k, 2) == 1, lax.div(k + 1, 2), ROWS - lax.div(k, 2))
        to_row(d).wait_recv()
        put_j(d, jbuf[d - 1])
        return _

    lax.fori_loop(1, ROWS, take_j, 0)

    def tiles(points_i, dirs_i, probs):
        left = i_operand(decode(points_i, factor))
        for n in range(ROWS * B // CHUNK):
            part = pl.ds(n * CHUNK, CHUNK)
            s = jnp.dot(left, jop[:, part], preferred_element_type=f32)
            probs[:, part] = jnp.exp2(s).astype(bf16)
        out = lax.dot_general(jdir[...], probs[...], (((1,), (1,)), ((), ())), preferred_element_type=f32)
        return out, jnp.dot(dirs_i, probs[...], preferred_element_type=f32)

    def to_owner(i):
        return pltpu.make_async_remote_copy(
            src_ref=obuf.at[i], dst_ref=cpart.at[i - 1], send_sem=osend, recv_sem=csem,
            device_id=col_peer(shift(i)), device_id_type=MESH)

    out, more = tiles(send[:F], send[F:] * bf16(0.5), probs.at[:B])
    obuf[0] = out * 0.5
    jacc[...] = more

    def take_i(q, _):
        i = 2 * q + 1
        to_col(i).wait_recv()
        to_col(i + 1).wait_recv()
        weight = jnp.where(q == HALF // 2 - 1, 0.5, 1.0)
        first, second = ibuf[i - 1], ibuf[i]
        halved = (second[F:].astype(f32) * weight).astype(bf16)
        out, more = tiles(
            jnp.concatenate([first[:F], second[:F]], axis=1),
            jnp.concatenate([first[F:], halved], axis=1), probs)
        obuf[i] = out[:, :B]
        obuf[i + 1] = out[:, B:] * weight
        jacc[...] += more
        to_owner(i).start()
        to_owner(i + 1).start()
        return _

    lax.fori_loop(0, HALF // 2, take_i, 0)

    def to_row_owner(d):
        return pltpu.make_async_remote_copy(
            src_ref=jacc.at[:, slot(d)], dst_ref=rpart.at[d - 1], send_sem=osend, recv_sem=rsem,
            device_id=row_peer(d), device_id_type=MESH)

    def push_j(d, _):
        to_row_owner(d).start()
        return _

    lax.fori_loop(1, ROWS, push_j, 0)

    res = residual[...]
    total = obuf[0] + jacc[:, :B] + noise[...] * dirs

    def whole(src, dst, s_sem, r_sem):
        return pltpu.make_async_remote_copy(
            src_ref=src, dst_ref=dst, send_sem=s_sem, recv_sem=r_sem,
            device_id=row_peer(1), device_id_type=MESH)

    whole(cpart, cpart, osend, csem).wait_recv()
    total += jnp.sum(cpart[...], axis=0)
    whole(rpart, rpart, osend, rsem).wait_recv()
    image = total + jnp.sum(rpart[...], axis=0)

    lane = lax.broadcasted_iota(jnp.int32, (R, B), 1)
    local = jnp.zeros((R, B), f32)
    for n, prod in enumerate((res * res, res * image, dirs * image, image * image)):
        local = jnp.where(lane == n, jnp.sum(prod, axis=1, keepdims=True), local)
    sums[...] = local

    def sum_to_col(d):
        return pltpu.make_async_remote_copy(
            src_ref=sums, dst_ref=csum.at[d - 1], send_sem=ssend, recv_sem=ssem,
            device_id=col_peer(d), device_id_type=MESH)

    def push_c(d, _):
        sum_to_col(d).start()
        return _

    lax.fori_loop(1, COLS, push_c, 0)
    whole(csum, csum, ssend, ssem).wait_recv()
    sums2[...] = sums[...] + jnp.sum(csum[...], axis=0)

    def sum_to_row(d):
        return pltpu.make_async_remote_copy(
            src_ref=sums2, dst_ref=rsum.at[d - 1], send_sem=ssend, recv_sem=ssem2,
            device_id=row_peer(d), device_id_type=MESH)

    def push_r(d, _):
        sum_to_row(d).start()
        return _

    lax.fori_loop(1, ROWS, push_r, 0)
    whole(rsum, rsum, ssend, ssem2).wait_recv()
    tot = sums2[...] + jnp.sum(rsum[...], axis=0)
    rr, rq, dq, qq = tot[:, 0:1], tot[:, 1:2], tot[:, 2:3], tot[:, 3:4]
    step = rr / dq
    nxt = rr - 2.0 * step * rq + step * (step * qq)
    res_next = res - step * image
    res_out[...] = res_next
    dir_out[...] = res_next + (nxt / rr) * dirs

    whole(jbuf, jbuf, send_sem, jsem.at[0]).wait_send()
    whole(ibuf, ibuf, send_sem, jsem.at[0]).wait_send()
    whole(cpart, cpart, osend, csem).wait_send()
    whole(rpart, rpart, osend, rsem).wait_send()
    whole(csum, csum, ssend, ssem).wait_send()
    whole(rsum, rsum, ssend, ssem2).wait_send()


def on_device(points, inv_scale, noise_var, residual, direction):
    vmem = pl.BlockSpec(memory_space=pltpu.VMEM)
    dma = pltpu.SemaphoreType.DMA
    out = jax.ShapeDtypeStruct((R, B), f32)
    return pl.pallas_call(
        kernel,
        out_shape=(out, out),
        in_specs=[vmem] * 5,
        out_specs=(vmem, vmem),
        scratch_shapes=[
            pltpu.VMEM((MSG, B), bf16),
            pltpu.VMEM((ROWS - 1, MSG, B), bf16),
            pltpu.VMEM((HALF, MSG, B), bf16),
            pltpu.VMEM((DEPTH, ROWS * B), bf16),
            pltpu.VMEM((R, ROWS * B), bf16),
            pltpu.VMEM((R, ROWS * B), f32),
            pltpu.VMEM((2 * B, ROWS * B), bf16),
            pltpu.VMEM((HALF + 1, R, B), f32),
            pltpu.VMEM((HALF, R, B), f32),
            pltpu.VMEM((ROWS - 1, R, B), f32),
            pltpu.VMEM((R, B), f32),
            pltpu.VMEM((COLS - 1, R, B), f32),
            pltpu.VMEM((R, B), f32),
            pltpu.VMEM((ROWS - 1, R, B), f32),
            dma, dma((ROWS - 1,)), dma((HALF,)), dma, dma, dma, dma, dma, dma,
        ],
        compiler_params=pltpu.CompilerParams(
            collective_id=0, has_side_effects=True, vmem_limit_bytes=32 << 20),
    )(points, inv_scale.reshape(1, F), noise_var.reshape(1, B), residual, direction)


def solution(mesh):
    split_points = P(None, ("row", "col"))
    return jax.shard_map(
        on_device,
        mesh=mesh,
        in_specs=(split_points, P(), P(("row", "col")), split_points, split_points),
        out_specs=(split_points, split_points),
        check_vma=False,
    )
```

```python
import functools
import math

import jax
import jax.numpy as jnp
from jax import lax
from jax.experimental import pallas as pl
from jax.experimental.pallas import tpu as pltpu
from jax.sharding import PartitionSpec as P

MESH = pl.DeviceIdType.MESH
F = 64
R = 16
B = 128
ROWS, COLS = 16, 32
HALF = COLS // 2
MSG = F + R
DEPTH = 256
KEEP = 48
GROUP, GROUPS = 4, 4
WIDTH = ROWS * B // 2
CHUNK = 512
CODE = 250.0 / 6.0
BIAS = 125.0
SQRT_LOG2E = math.sqrt(math.log2(math.e))
bf16, f32 = jnp.bfloat16, jnp.float32


def encode(x):
    mag = jnp.exp2(jnp.abs(x) * CODE - BIAS)
    return jnp.where(x < 0, -mag, mag).astype(bf16)


def decode(code, factor):
    y = code.astype(f32)
    mag = (jnp.log2(jnp.abs(y)) + BIAS) * factor
    return jnp.where(y < 0, -mag, mag)


def split(a):
    hi = a.astype(bf16)
    hi32 = hi.astype(f32)
    mid = (a - hi32).astype(bf16)
    mid32 = mid.astype(f32)
    norm = -jnp.sum(hi32 * (0.5 * hi32 + mid32), axis=0, keepdims=True)
    n0 = norm.astype(bf16).astype(f32)
    n1 = (norm - n0).astype(bf16).astype(f32)
    n2 = norm - n0 - n1
    return hi, mid, (n0, n1, n2)


def aux_rows(norms, first):
    row = lax.broadcasted_iota(jnp.int32, (16, norms[0].shape[1]), 0)
    out = jnp.where((row >= 3 - first) & (row < 6 - first), 1.0, 0.0)
    for i, n in enumerate(norms):
        out = jnp.where(row == first + i, n, out)
    return out.astype(bf16)


def j_operand(a):
    hi, mid, norms = split(a)
    return jnp.concatenate([hi, mid, hi, mid[:KEEP], aux_rows(norms, 3)], axis=0)


def i_operand(a):
    hi, mid, norms = split(a)
    return jnp.concatenate([hi, hi, mid, mid[:KEEP], aux_rows(norms, 0)], axis=0).T


def far_first(k, n):
    return jnp.where(lax.rem(k, 2) == 1, n // 2 - lax.div(k, 2), n // 2 + lax.div(k, 2))


def kernel(
    points_hbm, scale_hbm, noise_hbm, residual_hbm, direction_hbm, res_out, dir_out,
    points, scale, noise, residual, direction, send, jbuf, ibuf, jop, jdir, jacc, iop, idir, oown, own, probs, obuf, cpart, rpart, sums, csum, sums2, rsum,
    in_sem, send_sem, jsem, isem, osend, csem, rsem, ssend, ssem, ssem2,
):
    r, c = lax.axis_index("row"), lax.axis_index("col")

    def row_peer(d):
        return (lax.rem(r + d, ROWS), c)

    def col_peer(d):
        return (r, lax.rem(c + d + COLS, COLS))

    def shift(i):
        return jnp.where(lax.rem(i, 2) == 1, i, -i)

    staged = ((points_hbm, points), (scale_hbm, scale), (noise_hbm, noise), (residual_hbm, residual), (direction_hbm, direction))
    for n, (src, dst) in enumerate(staged):
        pltpu.make_async_copy(src, dst, in_sem.at[n]).start()

    barrier = pltpu.get_barrier_semaphore()

    def greet(k, _):
        @pl.when(k < ROWS)
        def _row():
            pl.semaphore_signal(barrier, inc=1, device_id=row_peer(far_first(k, ROWS)), device_id_type=MESH)
        i = HALF + 1 - k
        pl.semaphore_signal(barrier, inc=1, device_id=col_peer(shift(i)), device_id_type=MESH)
        return _

    lax.fori_loop(1, HALF + 1, greet, 0)

    for n, (src, dst) in enumerate(staged):
        pltpu.make_async_copy(src, dst, in_sem.at[n]).wait()
    dirs = direction[...]
    send[:F, :] = encode(points[...])
    send[F:, :] = dirs.astype(bf16)
    factor = jnp.broadcast_to(scale[...], (B, F)).T[:, :1] * (SQRT_LOG2E / CODE)

    pl.semaphore_wait(barrier, ROWS - 1 + HALF)

    def to_row(d):
        return pltpu.make_async_remote_copy(
            src_ref=send, dst_ref=jbuf.at[d - 1], send_sem=send_sem, recv_sem=jsem.at[d - 1],
            device_id=row_peer(ROWS - d), device_id_type=MESH)

    def to_col(i):
        return pltpu.make_async_remote_copy(
            src_ref=send, dst_ref=ibuf.at[i - 1], send_sem=send_sem, recv_sem=isem.at[i - 1],
            device_id=col_peer(-shift(i)), device_id_type=MESH)

    def near_first(p):
        return jnp.where(lax.rem(p, 2) == 1, lax.div(p + 1, 2), lax.rem(ROWS - lax.div(p, 2), ROWS))

    def push(k, _):
        @pl.when(k < ROWS)
        def _row():
            to_row(near_first(k)).start()
        to_col(k).start()
        return _

    lax.fori_loop(1, HALF + 1, push, 0)

    def slot(n):
        return pl.ds(pl.multiple_of(n * B, B), B)

    def put_j(p, msg):
        part, place = lax.div(p, ROWS // 2), slot(lax.rem(p, ROWS // 2))
        jop[part, :, place] = j_operand(decode(msg[:F], factor))
        jdir[part, :, place] = msg[F:]

    def take_j(p, _):
        d = near_first(p)
        to_row(d).wait_recv()
        put_j(p, jbuf[d - 1])
        return _

    def take_i(n, g):
        i = g * GROUP + n
        to_col(i + 1).wait_recv()
        msg = ibuf[i]
        weight = jnp.where(i == HALF - 1, 0.5, 1.0)
        iop[g, slot(n), :] = i_operand(decode(msg[:F], factor))
        idir[g, :, slot(n)] = (msg[F:].astype(f32) * weight).astype(bf16)
        return g

    def tile(left, dirs_i, h, probs):
        for n in range(WIDTH // CHUNK):
            part = pl.ds(n * CHUNK, CHUNK)
            s = jnp.dot(left, jop[h, :, part], preferred_element_type=f32)
            probs[:, part] = jnp.exp2(s).astype(bf16)
        jacc[h] += jnp.dot(dirs_i, probs[...], preferred_element_type=f32)
        return lax.dot_general(jdir[h], probs[...], (((1,), (1,)), ((), ())), preferred_element_type=f32)

    def to_owner(n, g):
        i = g * GROUP + n
        return pltpu.make_async_remote_copy(
            src_ref=obuf.at[g, :, slot(n)], dst_ref=cpart.at[i], send_sem=osend, recv_sem=csem,
            device_id=col_peer(shift(i + 1)), device_id_type=MESH)

    def push_o(n, g):
        to_owner(n, g).start()
        return g

    def to_row_owner(p):
        d = near_first(p)
        return pltpu.make_async_remote_copy(
            src_ref=jacc.at[lax.div(p, ROWS // 2), :, slot(lax.rem(p, ROWS // 2))], dst_ref=rpart.at[d - 1],
            send_sem=osend, recv_sem=rsem, device_id=row_peer(d), device_id_type=MESH)

    def push_j(p, _):
        to_row_owner(p).start()
        return _

    put_j(0, send[...])
    oown[...] = i_operand(decode(send[:F], factor))
    jacc[...] = jnp.zeros(jacc.shape, f32)
    obuf[...] = jnp.zeros(obuf.shape, f32)
    own[...] = jnp.zeros(own.shape, f32)

    def step_of(t, _):
        early = t < GROUPS
        g = jnp.where(early, lax.rem(t, 2), lax.div(t, 2))
        h = jnp.where(early, lax.div(t, 2), lax.rem(t, 2))

        @pl.when(early & (lax.rem(t, 2) == 0))
        def _half():
            lax.fori_loop(jnp.maximum(h * (ROWS // 2), 1), (h + 1) * (ROWS // 2), take_j, 0)
            own[...] += 0.5 * tile(oown[...], send[F:] * bf16(0.5), h, probs.at[:B])

        @pl.when(h == 0)
        def _group():
            lax.fori_loop(0, GROUP, take_i, g)

        obuf[g] += tile(iop[g], idir[g], h, probs)

        @pl.when(t == 2 * GROUPS - 1)
        def _last():
            obuf[g, :, slot(GROUP - 1)] = 0.5 * obuf[g, :, slot(GROUP - 1)]

        @pl.when(h == 1)
        def _rows_done():
            lax.fori_loop(0, GROUP, push_o, g)

        @pl.when(t >= 2 * GROUPS - 2)
        def _columns_done():
            lax.fori_loop(jnp.maximum(h * (ROWS // 2), 1), (h + 1) * (ROWS // 2), push_j, 0)
        return _

    lax.fori_loop(0, 2 * GROUPS, step_of, 0)

    res = residual[...]
    total = own[...] + jacc[0, :, :B] + noise[...] * dirs

    def whole(src, dst, s_sem, r_sem):
        return pltpu.make_async_remote_copy(
            src_ref=src, dst_ref=dst, send_sem=s_sem, recv_sem=r_sem,
            device_id=row_peer(1), device_id_type=MESH)

    whole(cpart, cpart, osend, csem).wait_recv()
    total += jnp.sum(cpart[...], axis=0)
    whole(rpart, rpart, osend, rsem).wait_recv()
    image = total + jnp.sum(rpart[...], axis=0)

    ahead = lax.broadcasted_iota(jnp.int32, (R, B), 1) - lax.broadcasted_iota(jnp.int32, (R, B), 0)
    local = jnp.zeros((R, B), f32)
    for n, prod in enumerate((res * res, res * image, dirs * image, image * image)):
        local = jnp.where(ahead == n * R, jnp.sum(prod, axis=1, keepdims=True), local)
    sums[...] = jnp.sum(local, axis=0, keepdims=True)

    def sum_to_col(d):
        return pltpu.make_async_remote_copy(
            src_ref=sums, dst_ref=csum.at[pl.ds(d - 1, 1)], send_sem=ssend, recv_sem=ssem,
            device_id=col_peer(d), device_id_type=MESH)

    def push_c(k, _):
        sum_to_col(far_first(k, COLS)).start()
        return _

    lax.fori_loop(1, COLS, push_c, 0)
    whole(csum, csum, ssend, ssem).wait_recv()
    sums2[...] = sums[...] + jnp.sum(csum[...], axis=0, keepdims=True)

    def sum_to_row(d):
        return pltpu.make_async_remote_copy(
            src_ref=sums2, dst_ref=rsum.at[pl.ds(d - 1, 1)], send_sem=ssend, recv_sem=ssem2,
            device_id=row_peer(d), device_id_type=MESH)

    def push_r(k, _):
        sum_to_row(far_first(k, ROWS)).start()
        return _

    lax.fori_loop(1, ROWS, push_r, 0)
    whole(rsum, rsum, ssend, ssem2).wait_recv()
    tot = sums2[...] + jnp.sum(rsum[...], axis=0, keepdims=True)
    rr, rq, dq, qq = (jnp.sum(jnp.where(ahead == n * R, tot, 0.0), axis=1, keepdims=True) for n in range(4))
    step = rr / dq
    nxt = rr - 2.0 * step * rq + step * (step * qq)
    res_next = res - step * image
    res_out[...] = res_next
    dir_out[...] = res_next + (nxt / rr) * dirs

    whole(jbuf, jbuf, send_sem, jsem.at[0]).wait_send()
    whole(ibuf, ibuf, send_sem, jsem.at[0]).wait_send()
    whole(cpart, cpart, osend, csem).wait_send()
    whole(rpart, rpart, osend, rsem).wait_send()
    whole(csum, csum, ssend, ssem).wait_send()
    whole(rsum, rsum, ssend, ssem2).wait_send()


def on_device(points, inv_scale, noise_var, residual, direction):
    vmem = pl.BlockSpec(memory_space=pltpu.VMEM)
    dma = pltpu.SemaphoreType.DMA
    out = jax.ShapeDtypeStruct((R, B), f32)
    return pl.pallas_call(
        kernel,
        out_shape=(out, out),
        in_specs=[pl.BlockSpec(memory_space=pltpu.HBM)] * 5,
        out_specs=(vmem, vmem),
        scratch_shapes=[
            pltpu.VMEM((F, B), f32),
            pltpu.VMEM((1, F), f32),
            pltpu.VMEM((1, B), f32),
            pltpu.VMEM((R, B), f32),
            pltpu.VMEM((R, B), f32),
            pltpu.VMEM((MSG, B), bf16),
            pltpu.VMEM((ROWS - 1, MSG, B), bf16),
            pltpu.VMEM((HALF, MSG, B), bf16),
            pltpu.VMEM((2, DEPTH, WIDTH), bf16),
            pltpu.VMEM((2, R, WIDTH), bf16),
            pltpu.VMEM((2, R, WIDTH), f32),
            pltpu.VMEM((GROUPS, GROUP * B, DEPTH), bf16),
            pltpu.VMEM((GROUPS, R, GROUP * B), bf16),
            pltpu.VMEM((B, DEPTH), bf16),
            pltpu.VMEM((R, B), f32),
            pltpu.VMEM((GROUP * B, WIDTH), bf16),
            pltpu.VMEM((GROUPS, R, GROUP * B), f32),
            pltpu.VMEM((HALF, R, B), f32),
            pltpu.VMEM((ROWS - 1, R, B), f32),
            pltpu.VMEM((1, B), f32),
            pltpu.VMEM((COLS - 1, B), f32),
            pltpu.VMEM((1, B), f32),
            pltpu.VMEM((ROWS - 1, B), f32),
            dma((5,)), dma, dma((ROWS - 1,)), dma((HALF,)), dma, dma, dma, dma, dma, dma,
        ],
        compiler_params=pltpu.CompilerParams(
            collective_id=0, has_side_effects=True, vmem_limit_bytes=60 << 20),
    )(points, inv_scale.reshape(1, F), noise_var.reshape(1, B), residual, direction)


def solution(mesh):
    split_points = P(None, ("row", "col"))
    return jax.shard_map(
        on_device,
        mesh=mesh,
        in_specs=(split_points, P(), P(("row", "col")), split_points, split_points),
        out_specs=(split_points, split_points),
        check_vma=False,
    )
```

```python
import functools
import math

import jax
import jax.numpy as jnp
from jax import lax
from jax.experimental import pallas as pl
from jax.experimental.pallas import tpu as pltpu
from jax.sharding import PartitionSpec as P

MESH = pl.DeviceIdType.MESH
F = 64
R = 16
B = 128
ROWS, COLS = 16, 32
HALF = COLS // 2
MSG = F + R
DEPTH = 256
KEEP = 48
GROUP, GROUPS = 4, 4
WIDTH = ROWS * B // 2
CHUNK = 512
CODE = 250.0 / 6.0
BIAS = 125.0
SQRT_LOG2E = math.sqrt(math.log2(math.e))
bf16, f32 = jnp.bfloat16, jnp.float32


def encode(x):
    mag = jnp.exp2(jnp.abs(x) * CODE - BIAS)
    return jnp.where(x < 0, -mag, mag).astype(bf16)


def decode(code, factor):
    y = code.astype(f32)
    mag = (jnp.log2(jnp.abs(y)) + BIAS) * factor
    return jnp.where(y < 0, -mag, mag)


def split(a):
    hi = a.astype(bf16)
    hi32 = hi.astype(f32)
    mid = (a - hi32).astype(bf16)
    mid32 = mid.astype(f32)
    norm = -jnp.sum(hi32 * (0.5 * hi32 + mid32), axis=0, keepdims=True)
    n0 = norm.astype(bf16).astype(f32)
    n1 = (norm - n0).astype(bf16).astype(f32)
    n2 = norm - n0 - n1
    return hi, mid, (n0, n1, n2)


def aux_rows(norms, first):
    row = lax.broadcasted_iota(jnp.int32, (16, norms[0].shape[1]), 0)
    out = jnp.where((row >= 3 - first) & (row < 6 - first), 1.0, 0.0)
    for i, n in enumerate(norms):
        out = jnp.where(row == first + i, n, out)
    return out.astype(bf16)


def j_operand(a):
    hi, mid, norms = split(a)
    return jnp.concatenate([hi, mid, hi, mid[:KEEP], aux_rows(norms, 3)], axis=0)


def i_operand(a):
    hi, mid, norms = split(a)
    return jnp.concatenate([hi, hi, mid, mid[:KEEP], aux_rows(norms, 0)], axis=0).T


def far_first(k, n):
    return jnp.where(lax.rem(k, 2) == 1, n // 2 - lax.div(k, 2), n // 2 + lax.div(k, 2))


def kernel(
    points_hbm, scale_hbm, noise_hbm, residual_hbm, direction_hbm, out,
    points, scale, noise, residual, direction, send, jbuf, ibuf, jop, jdir, jacc, iop, idir, oown, own, probs, obuf, cpart, rpart, sums, csum, sums2, rsum,
    in_sem, send_sem, jsem, isem, osend, csem, rsem, ssend, ssem, ssem2,
):
    r, c = lax.axis_index("row"), lax.axis_index("col")

    def row_peer(d):
        return (lax.rem(r + d, ROWS), c)

    def col_peer(d):
        return (r, lax.rem(c + d + COLS, COLS))

    def shift(i):
        return jnp.where(lax.rem(i, 2) == 1, i, -i)

    staged = ((points_hbm, points), (scale_hbm, scale), (noise_hbm, noise), (residual_hbm, residual), (direction_hbm, direction))
    for n, (src, dst) in enumerate(staged):
        pltpu.make_async_copy(src, dst, in_sem.at[n]).start()

    barrier = pltpu.get_barrier_semaphore()

    def greet(k, _):
        @pl.when(k < ROWS)
        def _row():
            pl.semaphore_signal(barrier, inc=1, device_id=row_peer(far_first(k, ROWS)), device_id_type=MESH)
        i = HALF + 1 - k
        pl.semaphore_signal(barrier, inc=1, device_id=col_peer(shift(i)), device_id_type=MESH)
        return _

    lax.fori_loop(1, HALF + 1, greet, 0)

    for n, (src, dst) in enumerate(staged):
        pltpu.make_async_copy(src, dst, in_sem.at[n]).wait()
    dirs = direction[...]
    send[:F, :] = encode(points[...])
    send[F:, :] = dirs.astype(bf16)
    factor = jnp.broadcast_to(scale[...], (B, F)).T[:, :1] * (SQRT_LOG2E / CODE)

    pl.semaphore_wait(barrier, ROWS - 1 + HALF)

    def near_first(p):
        return jnp.where(lax.rem(p, 2) == 1, lax.div(p + 1, 2), lax.rem(ROWS - lax.div(p, 2), ROWS))

    def to_row(p):
        return pltpu.make_async_remote_copy(
            src_ref=send, dst_ref=jbuf.at[p], send_sem=send_sem, recv_sem=jsem.at[p],
            device_id=row_peer(ROWS - near_first(p)), device_id_type=MESH)

    def to_col(i):
        return pltpu.make_async_remote_copy(
            src_ref=send, dst_ref=ibuf.at[i - 1], send_sem=send_sem, recv_sem=isem.at[i - 1],
            device_id=col_peer(-shift(i)), device_id_type=MESH)

    def push(k, _):
        @pl.when(k < ROWS)
        def _row():
            to_row(k).start()
        to_col(k).start()
        return _

    lax.fori_loop(1, HALF + 1, push, 0)

    def slot(n):
        return pl.ds(pl.multiple_of(n * B, B), B)

    def side_by_side(blocks):
        return jnp.concatenate(blocks, axis=1)

    def take_j(q, _):
        for n in range(GROUP):
            @pl.when(q * GROUP + n > 0)
            def _arrived():
                to_row(q * GROUP + n).wait_recv()
        part = lax.div(q, 2)
        place = pl.ds(pl.multiple_of(lax.rem(q, 2) * GROUP * B, GROUP * B), GROUP * B)
        blocks = [jbuf[q * GROUP + n] for n in range(GROUP)]
        jop[part, :, place] = j_operand(decode(side_by_side([m[:F] for m in blocks]), factor))
        jdir[part, :, place] = side_by_side([m[F:] for m in blocks])
        return _

    def take_i(g):
        for n in range(GROUP):
            to_col(g * GROUP + n + 1).wait_recv()
        weight = jnp.where(g == GROUPS - 1, 0.5, 1.0)
        blocks = [ibuf[g * GROUP + n] for n in range(GROUP)]
        iop[g] = i_operand(decode(side_by_side([m[:F] for m in blocks]), factor))
        last = (blocks[-1][F:].astype(f32) * weight).astype(bf16)
        idir[g] = side_by_side([m[F:] for m in blocks[:-1]] + [last])

    def tile(left, dirs_i, h, probs):
        for n in range(WIDTH // CHUNK):
            part = pl.ds(n * CHUNK, CHUNK)
            s = jnp.dot(left, jop[h, :, part], preferred_element_type=f32)
            probs[:, part] = jnp.exp2(s).astype(bf16)
        jacc[h] += jnp.dot(dirs_i, probs[...], preferred_element_type=f32)
        return lax.dot_general(jdir[h], probs[...], (((1,), (1,)), ((), ())), preferred_element_type=f32)

    def to_owner(n, g):
        i = g * GROUP + n
        return pltpu.make_async_remote_copy(
            src_ref=obuf.at[g, :, slot(n)], dst_ref=cpart.at[i], send_sem=osend, recv_sem=csem,
            device_id=col_peer(shift(i + 1)), device_id_type=MESH)

    def push_o(n, g):
        to_owner(n, g).start()
        return g

    def to_row_owner(p):
        d = near_first(p)
        return pltpu.make_async_remote_copy(
            src_ref=jacc.at[lax.div(p, ROWS // 2), :, slot(lax.rem(p, ROWS // 2))], dst_ref=rpart.at[d - 1],
            send_sem=osend, recv_sem=rsem, device_id=row_peer(d), device_id_type=MESH)

    def push_j(p, _):
        to_row_owner(p).start()
        return _

    jbuf[0] = send[...]
    oown[...] = i_operand(decode(send[:F], factor))
    jacc[...] = jnp.zeros(jacc.shape, f32)
    obuf[...] = jnp.zeros(obuf.shape, f32)
    own[...] = jnp.zeros(own.shape, f32)

    def step_of(t, _):
        early = t < GROUPS
        g = jnp.where(early, lax.rem(t, 2), lax.div(t, 2))
        h = jnp.where(early, lax.div(t, 2), lax.rem(t, 2))

        @pl.when(early & (lax.rem(t, 2) == 0))
        def _half():
            lax.fori_loop(2 * h, 2 * h + 2, take_j, 0)
            own[...] += 0.5 * tile(oown[...], send[F:] * bf16(0.5), h, probs.at[:B])

        @pl.when(h == 0)
        def _group():
            take_i(g)

        obuf[g] += tile(iop[g], idir[g], h, probs)

        @pl.when(t == 2 * GROUPS - 1)
        def _last():
            obuf[g, :, slot(GROUP - 1)] = 0.5 * obuf[g, :, slot(GROUP - 1)]

        @pl.when(h == 1)
        def _rows_done():
            lax.fori_loop(0, GROUP, push_o, g)

        @pl.when(t >= 2 * GROUPS - 2)
        def _columns_done():
            lax.fori_loop(jnp.maximum(h * (ROWS // 2), 1), (h + 1) * (ROWS // 2), push_j, 0)
        return _

    lax.fori_loop(0, 2 * GROUPS, step_of, 0)

    res = residual[...]
    total = own[...] + jacc[0, :, :B] + noise[...] * dirs

    def whole(src, dst, s_sem, r_sem):
        return pltpu.make_async_remote_copy(
            src_ref=src, dst_ref=dst, send_sem=s_sem, recv_sem=r_sem,
            device_id=row_peer(1), device_id_type=MESH)

    whole(cpart, cpart, osend, csem).wait_recv()
    total += jnp.sum(cpart[...], axis=0)
    whole(rpart, rpart, osend, rsem).wait_recv()
    image = total + jnp.sum(rpart[...], axis=0)

    ahead = lax.broadcasted_iota(jnp.int32, (R, B), 1) - lax.broadcasted_iota(jnp.int32, (R, B), 0)
    local = jnp.zeros((R, B), f32)
    for n, prod in enumerate((res * res, res * image, dirs * image, image * image)):
        local = jnp.where(ahead == n * R, jnp.sum(prod, axis=1, keepdims=True), local)
    sums[...] = jnp.sum(local, axis=0, keepdims=True)

    def sum_to_col(d):
        return pltpu.make_async_remote_copy(
            src_ref=sums, dst_ref=csum.at[pl.ds(d - 1, 1)], send_sem=ssend, recv_sem=ssem,
            device_id=col_peer(d), device_id_type=MESH)

    def push_c(k, _):
        sum_to_col(far_first(k, COLS)).start()
        return _

    lax.fori_loop(1, COLS, push_c, 0)
    whole(csum, csum, ssend, ssem).wait_recv()
    sums2[...] = sums[...] + jnp.sum(csum[...], axis=0, keepdims=True)

    def sum_to_row(d):
        return pltpu.make_async_remote_copy(
            src_ref=sums2, dst_ref=rsum.at[pl.ds(d - 1, 1)], send_sem=ssend, recv_sem=ssem2,
            device_id=row_peer(d), device_id_type=MESH)

    def push_r(k, _):
        sum_to_row(far_first(k, ROWS)).start()
        return _

    lax.fori_loop(1, ROWS, push_r, 0)
    whole(rsum, rsum, ssend, ssem2).wait_recv()
    tot = sums2[...] + jnp.sum(rsum[...], axis=0, keepdims=True)
    rr, rq, dq, qq = (jnp.sum(jnp.where(ahead == n * R, tot, 0.0), axis=1, keepdims=True) for n in range(4))
    step = rr / dq
    nxt = rr - 2.0 * step * rq + step * (step * qq)
    out[:R, :] = image
    out[R:2 * R, :] = jnp.broadcast_to(step, (R, B))
    out[2 * R:, :] = jnp.broadcast_to(nxt / rr, (R, B))

    whole(jbuf.at[pl.ds(1, ROWS - 1)], jbuf.at[pl.ds(1, ROWS - 1)], send_sem, jsem.at[0]).wait_send()
    whole(ibuf, ibuf, send_sem, jsem.at[0]).wait_send()
    whole(cpart, cpart, osend, csem).wait_send()
    whole(rpart, rpart, osend, rsem).wait_send()
    whole(csum, csum, ssend, ssem).wait_send()
    whole(rsum, rsum, ssend, ssem2).wait_send()


def on_device(points, inv_scale, noise_var, residual, direction):
    vmem = pl.BlockSpec(memory_space=pltpu.VMEM)
    dma = pltpu.SemaphoreType.DMA
    found = pl.pallas_call(
        kernel,
        out_shape=jax.ShapeDtypeStruct((3 * R, B), f32),
        in_specs=[pl.BlockSpec(memory_space=pltpu.HBM)] * 5,
        out_specs=vmem,
        scratch_shapes=[
            pltpu.VMEM((F, B), f32),
            pltpu.VMEM((1, F), f32),
            pltpu.VMEM((1, B), f32),
            pltpu.VMEM((R, B), f32),
            pltpu.VMEM((R, B), f32),
            pltpu.VMEM((MSG, B), bf16),
            pltpu.VMEM((ROWS, MSG, B), bf16),
            pltpu.VMEM((HALF, MSG, B), bf16),
            pltpu.VMEM((2, DEPTH, WIDTH), bf16),
            pltpu.VMEM((2, R, WIDTH), bf16),
            pltpu.VMEM((2, R, WIDTH), f32),
            pltpu.VMEM((GROUPS, GROUP * B, DEPTH), bf16),
            pltpu.VMEM((GROUPS, R, GROUP * B), bf16),
            pltpu.VMEM((B, DEPTH), bf16),
            pltpu.VMEM((R, B), f32),
            pltpu.VMEM((GROUP * B, WIDTH), bf16),
            pltpu.VMEM((GROUPS, R, GROUP * B), f32),
            pltpu.VMEM((HALF, R, B), f32),
            pltpu.VMEM((ROWS - 1, R, B), f32),
            pltpu.VMEM((1, B), f32),
            pltpu.VMEM((COLS - 1, B), f32),
            pltpu.VMEM((1, B), f32),
            pltpu.VMEM((ROWS - 1, B), f32),
            dma((5,)), dma, dma((ROWS,)), dma((HALF,)), dma, dma, dma, dma, dma, dma,
        ],
        compiler_params=pltpu.CompilerParams(
            collective_id=0, has_side_effects=True, vmem_limit_bytes=60 << 20),
    )(points, inv_scale.reshape(1, F), noise_var.reshape(1, B), residual, direction)
    image, step, ratio = found[:R], found[R:2 * R], found[2 * R:]
    residual_next = residual - step * image
    return residual_next, residual_next + ratio * direction


def solution(mesh):
    split_points = P(None, ("row", "col"))
    return jax.shard_map(
        on_device,
        mesh=mesh,
        in_specs=(split_points, P(), P(("row", "col")), split_points, split_points),
        out_specs=(split_points, split_points),
        check_vma=False,
    )
```

```python
import functools
import math

import jax
import jax.numpy as jnp
from jax import lax
from jax.experimental import pallas as pl
from jax.experimental.pallas import tpu as pltpu
from jax.sharding import PartitionSpec as P

MESH = pl.DeviceIdType.MESH
F = 64
R = 16
B = 128
ROWS, COLS = 16, 32
HALF = COLS // 2
MSG = F + R
DEPTH = 256
KEEP = 48
GROUP, GROUPS = 4, 4
WIDTH = ROWS * B // 2
CHUNK = 512
CODE = 250.0 / 6.0
BIAS = 125.0
SQRT_LOG2E = math.sqrt(math.log2(math.e))
bf16, f32 = jnp.bfloat16, jnp.float32


def encode(x):
    mag = jnp.exp2(jnp.abs(x) * CODE - BIAS)
    return jnp.where(x < 0, -mag, mag).astype(bf16)


def decode(code, factor):
    y = code.astype(f32)
    mag = (jnp.log2(jnp.abs(y)) + BIAS) * factor
    return jnp.where(y < 0, -mag, mag)


def split(a):
    hi = a.astype(bf16)
    hi32 = hi.astype(f32)
    mid = (a - hi32).astype(bf16)
    mid32 = mid.astype(f32)
    norm = -jnp.sum(hi32 * (0.5 * hi32 + mid32), axis=0, keepdims=True)
    n0 = norm.astype(bf16).astype(f32)
    n1 = (norm - n0).astype(bf16).astype(f32)
    n2 = norm - n0 - n1
    return hi, mid, (n0, n1, n2)


def aux_rows(norms, first):
    row = lax.broadcasted_iota(jnp.int32, (16, norms[0].shape[1]), 0)
    out = jnp.where((row >= 3 - first) & (row < 6 - first), 1.0, 0.0)
    for i, n in enumerate(norms):
        out = jnp.where(row == first + i, n, out)
    return out.astype(bf16)


def j_operand(a):
    hi, mid, norms = split(a)
    return jnp.concatenate([hi, mid, hi, mid[:KEEP], aux_rows(norms, 3)], axis=0)


def i_operand(a):
    hi, mid, norms = split(a)
    return jnp.concatenate([hi, hi, mid, mid[:KEEP], aux_rows(norms, 0)], axis=0).T


def far_first(k, n):
    return jnp.where(lax.rem(k, 2) == 1, n // 2 - lax.div(k, 2), n // 2 + lax.div(k, 2))


def kernel(
    points_hbm, scale_hbm, noise_hbm, residual_hbm, direction_hbm, out,
    points, scale, noise, residual, direction, send, jbuf, ibuf, jop, jdir, jacc, iop, idir, oown, own, probs, obuf, cpart, rpart, sums, csum, sums2, rsum,
    in_sem, send_sem, jsem, isem, osend, csem, rsem, ssend, ssem, ssem2,
):
    r, c = lax.axis_index("row"), lax.axis_index("col")

    def row_peer(d):
        return (lax.rem(r + d, ROWS), c)

    def col_peer(d):
        return (r, lax.rem(c + d + COLS, COLS))

    def shift(i):
        d = HALF + 1 - i
        return jnp.where(lax.rem(d, 2) == 1, d, -d)

    staged = ((points_hbm, points), (scale_hbm, scale), (noise_hbm, noise), (residual_hbm, residual), (direction_hbm, direction))
    for n, (src, dst) in enumerate(staged):
        pltpu.make_async_copy(src, dst, in_sem.at[n]).start()

    barrier = pltpu.get_barrier_semaphore()

    def greet(k, _):
        @pl.when(k < ROWS)
        def _row():
            pl.semaphore_signal(barrier, inc=1, device_id=row_peer(far_first(k, ROWS)), device_id_type=MESH)
        pl.semaphore_signal(barrier, inc=1, device_id=col_peer(shift(k)), device_id_type=MESH)
        return _

    lax.fori_loop(1, HALF + 1, greet, 0, unroll=True)

    for n, (src, dst) in enumerate(staged):
        pltpu.make_async_copy(src, dst, in_sem.at[n]).wait()
    dirs = direction[...]
    send[:F, :] = encode(points[...])
    send[F:, :] = dirs.astype(bf16)
    factor = jnp.broadcast_to(scale[...], (B, F)).T[:, :1] * (SQRT_LOG2E / CODE)

    pl.semaphore_wait(barrier, ROWS - 1 + HALF)

    def to_row(p):
        return pltpu.make_async_remote_copy(
            src_ref=send, dst_ref=jbuf.at[p], send_sem=send_sem, recv_sem=jsem.at[p],
            device_id=row_peer(ROWS - far_first(p, ROWS)), device_id_type=MESH)

    def to_col(i):
        return pltpu.make_async_remote_copy(
            src_ref=send, dst_ref=ibuf.at[i - 1], send_sem=send_sem, recv_sem=isem.at[i - 1],
            device_id=col_peer(-shift(i)), device_id_type=MESH)

    def push(k, _):
        @pl.when(k < ROWS)
        def _row():
            to_row(k).start()
        to_col(k).start()
        return _

    lax.fori_loop(1, HALF + 1, push, 0, unroll=True)

    def slot(n):
        return pl.ds(pl.multiple_of(n * B, B), B)

    def side_by_side(blocks):
        return jnp.concatenate(blocks, axis=1)

    def take_j(q, _):
        for n in range(GROUP):
            @pl.when(q * GROUP + n > 0)
            def _arrived():
                to_row(q * GROUP + n).wait_recv()
        part = lax.div(q, 2)
        place = pl.ds(pl.multiple_of(lax.rem(q, 2) * GROUP * B, GROUP * B), GROUP * B)
        blocks = [jbuf[q * GROUP + n] for n in range(GROUP)]
        jop[part, :, place] = j_operand(decode(side_by_side([m[:F] for m in blocks]), factor))
        jdir[part, :, place] = side_by_side([m[F:] for m in blocks])
        return _

    def take_i(g):
        for n in range(GROUP):
            to_col(g * GROUP + n + 1).wait_recv()
        weight = jnp.where(g == 0, 0.5, 1.0)
        blocks = [ibuf[g * GROUP + n] for n in range(GROUP)]
        iop[g] = i_operand(decode(side_by_side([m[:F] for m in blocks]), factor))
        first = (blocks[0][F:].astype(f32) * weight).astype(bf16)
        idir[g] = side_by_side([first] + [m[F:] for m in blocks[1:]])

    def tile(left, dirs_i, h, probs):
        for n in range(WIDTH // CHUNK):
            part = pl.ds(n * CHUNK, CHUNK)
            s = jnp.dot(left, jop[h, :, part], preferred_element_type=f32)
            probs[:, part] = jnp.exp2(s).astype(bf16)
        jacc[h] += jnp.dot(dirs_i, probs[...], preferred_element_type=f32)
        return lax.dot_general(jdir[h], probs[...], (((1,), (1,)), ((), ())), preferred_element_type=f32)

    def to_owner(n, g):
        i = g * GROUP + n
        return pltpu.make_async_remote_copy(
            src_ref=obuf.at[g, :, slot(n)], dst_ref=cpart.at[i], send_sem=osend, recv_sem=csem,
            device_id=col_peer(shift(i + 1)), device_id_type=MESH)

    def push_o(n, g):
        to_owner(n, g).start()
        return g

    def to_row_owner(p):
        d = far_first(p, ROWS)
        return pltpu.make_async_remote_copy(
            src_ref=jacc.at[lax.div(p, ROWS // 2), :, slot(lax.rem(p, ROWS // 2))], dst_ref=rpart.at[d - 1],
            send_sem=osend, recv_sem=rsem, device_id=row_peer(d), device_id_type=MESH)

    def push_j(p, _):
        to_row_owner(p).start()
        return _

    jbuf[0] = send[...]
    oown[...] = i_operand(decode(send[:F], factor))
    jacc[...] = jnp.zeros(jacc.shape, f32)
    obuf[...] = jnp.zeros(obuf.shape, f32)
    own[...] = jnp.zeros(own.shape, f32)

    def step_of(t, _):
        g, h = lax.rem(t, GROUPS), lax.div(t, GROUPS)

        @pl.when(g == 0)
        def _half():
            lax.fori_loop(2 * h, 2 * h + 2, take_j, 0)
            own[...] += 0.5 * tile(oown[...], send[F:] * bf16(0.5), h, probs.at[:B])

        @pl.when(h == 0)
        def _group():
            take_i(g)

        obuf[g] += tile(iop[g], idir[g], h, probs)

        @pl.when(t == GROUPS)
        def _half_weight():
            obuf[0, :, :B] = 0.5 * obuf[0, :, :B]

        @pl.when(h == 1)
        def _rows_done():
            lax.fori_loop(0, GROUP, push_o, g)

        @pl.when(g == GROUPS - 1)
        def _columns_done():
            lax.fori_loop(jnp.maximum(h * (ROWS // 2), 1), (h + 1) * (ROWS // 2), push_j, 0)
        return _

    lax.fori_loop(0, 2 * GROUPS, step_of, 0)

    res = residual[...]
    total = own[...] + jacc[0, :, :B] + noise[...] * dirs

    def whole(src, dst, s_sem, r_sem):
        return pltpu.make_async_remote_copy(
            src_ref=src, dst_ref=dst, send_sem=s_sem, recv_sem=r_sem,
            device_id=row_peer(1), device_id_type=MESH)

    whole(cpart, cpart, osend, csem).wait_recv()
    total += jnp.sum(cpart[...], axis=0)
    whole(rpart, rpart, osend, rsem).wait_recv()
    image = total + jnp.sum(rpart[...], axis=0)

    ahead = lax.broadcasted_iota(jnp.int32, (R, B), 1) - lax.broadcasted_iota(jnp.int32, (R, B), 0)
    local = jnp.zeros((R, B), f32)
    for n, prod in enumerate((res * res, res * image, dirs * image, image * image)):
        local = jnp.where(ahead == n * R, jnp.sum(prod, axis=1, keepdims=True), local)
    sums[...] = jnp.sum(local, axis=0, keepdims=True)

    def sum_to_col(d):
        return pltpu.make_async_remote_copy(
            src_ref=sums, dst_ref=csum.at[pl.ds(d - 1, 1)], send_sem=ssend, recv_sem=ssem,
            device_id=col_peer(d), device_id_type=MESH)

    def push_c(k, _):
        sum_to_col(far_first(k, COLS)).start()
        return _

    lax.fori_loop(1, COLS, push_c, 0, unroll=True)
    whole(csum, csum, ssend, ssem).wait_recv()
    sums2[...] = sums[...] + jnp.sum(csum[...], axis=0, keepdims=True)

    def sum_to_row(d):
        return pltpu.make_async_remote_copy(
            src_ref=sums2, dst_ref=rsum.at[pl.ds(d - 1, 1)], send_sem=ssend, recv_sem=ssem2,
            device_id=row_peer(d), device_id_type=MESH)

    def push_r(k, _):
        sum_to_row(far_first(k, ROWS)).start()
        return _

    lax.fori_loop(1, ROWS, push_r, 0, unroll=True)
    whole(rsum, rsum, ssend, ssem2).wait_recv()
    tot = sums2[...] + jnp.sum(rsum[...], axis=0, keepdims=True)
    rr, rq, dq, qq = (jnp.sum(jnp.where(ahead == n * R, tot, 0.0), axis=1, keepdims=True) for n in range(4))
    step = rr / dq
    nxt = rr - 2.0 * step * rq + step * (step * qq)
    out[:R, :] = image
    out[R:2 * R, :] = jnp.broadcast_to(step, (R, B))
    out[2 * R:, :] = jnp.broadcast_to(nxt / rr, (R, B))

    whole(jbuf.at[pl.ds(1, ROWS - 1)], jbuf.at[pl.ds(1, ROWS - 1)], send_sem, jsem.at[0]).wait_send()
    whole(ibuf, ibuf, send_sem, jsem.at[0]).wait_send()
    whole(cpart, cpart, osend, csem).wait_send()
    whole(rpart, rpart, osend, rsem).wait_send()
    whole(csum, csum, ssend, ssem).wait_send()
    whole(rsum, rsum, ssend, ssem2).wait_send()


def on_device(points, inv_scale, noise_var, residual, direction):
    vmem = pl.BlockSpec(memory_space=pltpu.VMEM)
    dma = pltpu.SemaphoreType.DMA
    found = pl.pallas_call(
        kernel,
        out_shape=jax.ShapeDtypeStruct((3 * R, B), f32),
        in_specs=[pl.BlockSpec(memory_space=pltpu.HBM)] * 5,
        out_specs=vmem,
        scratch_shapes=[
            pltpu.VMEM((F, B), f32),
            pltpu.VMEM((1, F), f32),
            pltpu.VMEM((1, B), f32),
            pltpu.VMEM((R, B), f32),
            pltpu.VMEM((R, B), f32),
            pltpu.VMEM((MSG, B), bf16),
            pltpu.VMEM((ROWS, MSG, B), bf16),
            pltpu.VMEM((HALF, MSG, B), bf16),
            pltpu.VMEM((2, DEPTH, WIDTH), bf16),
            pltpu.VMEM((2, R, WIDTH), bf16),
            pltpu.VMEM((2, R, WIDTH), f32),
            pltpu.VMEM((GROUPS, GROUP * B, DEPTH), bf16),
            pltpu.VMEM((GROUPS, R, GROUP * B), bf16),
            pltpu.VMEM((B, DEPTH), bf16),
            pltpu.VMEM((R, B), f32),
            pltpu.VMEM((GROUP * B, WIDTH), bf16),
            pltpu.VMEM((GROUPS, R, GROUP * B), f32),
            pltpu.VMEM((HALF, R, B), f32),
            pltpu.VMEM((ROWS - 1, R, B), f32),
            pltpu.VMEM((1, B), f32),
            pltpu.VMEM((COLS - 1, B), f32),
            pltpu.VMEM((1, B), f32),
            pltpu.VMEM((ROWS - 1, B), f32),
            dma((5,)), dma, dma((ROWS,)), dma((HALF,)), dma, dma, dma, dma, dma, dma,
        ],
        compiler_params=pltpu.CompilerParams(
            collective_id=0, has_side_effects=True, vmem_limit_bytes=60 << 20),
    )(points, inv_scale.reshape(1, F), noise_var.reshape(1, B), residual, direction)
    image, step, ratio = found[:R], found[R:2 * R], found[2 * R:]
    residual_next = residual - step * image
    return residual_next, residual_next + ratio * direction


def solution(mesh):
    split_points = P(None, ("row", "col"))
    return jax.shard_map(
        on_device,
        mesh=mesh,
        in_specs=(split_points, P(), P(("row", "col")), split_points, split_points),
        out_specs=(split_points, split_points),
        check_vma=False,
    )
```

```python
import functools
import math

import jax
import jax.numpy as jnp
from jax import lax
from jax.experimental import pallas as pl
from jax.experimental.pallas import tpu as pltpu
from jax.sharding import PartitionSpec as P

MESH = pl.DeviceIdType.MESH
F = 64
R = 16
B = 128
ROWS, COLS = 16, 32
HALF = COLS // 2
MSG = F + R
DEPTH = 256
KEEP = 48
GROUP, GROUPS = 4, 4
WIDTH = ROWS * B // 2
CHUNK = 512
CODE = 250.0 / 6.0
BIAS = 125.0
SQRT_LOG2E = math.sqrt(math.log2(math.e))
bf16, f32 = jnp.bfloat16, jnp.float32


def encode(x):
    mag = jnp.exp2(jnp.abs(x) * CODE - BIAS)
    return jnp.where(x < 0, -mag, mag).astype(bf16)


def decode(code, factor):
    y = code.astype(f32)
    mag = (jnp.log2(jnp.abs(y)) + BIAS) * factor
    return jnp.where(y < 0, -mag, mag)


def split(a):
    hi = a.astype(bf16)
    hi32 = hi.astype(f32)
    mid = (a - hi32).astype(bf16)
    mid32 = mid.astype(f32)
    norm = -jnp.sum(hi32 * (0.5 * hi32 + mid32), axis=0, keepdims=True)
    n0 = norm.astype(bf16).astype(f32)
    n1 = (norm - n0).astype(bf16).astype(f32)
    n2 = norm - n0 - n1
    return hi, mid, (n0, n1, n2)


def aux_rows(norms, first):
    row = lax.broadcasted_iota(jnp.int32, (16, norms[0].shape[1]), 0)
    out = jnp.where((row >= 3 - first) & (row < 6 - first), 1.0, 0.0)
    for i, n in enumerate(norms):
        out = jnp.where(row == first + i, n, out)
    return out.astype(bf16)


def j_operand(a):
    hi, mid, norms = split(a)
    return jnp.concatenate([hi, mid, hi, mid[:KEEP], aux_rows(norms, 3)], axis=0)


def i_operand(a):
    hi, mid, norms = split(a)
    return jnp.concatenate([hi, hi, mid, mid[:KEEP], aux_rows(norms, 0)], axis=0).T


def far_first(k, n):
    return jnp.where(lax.rem(k, 2) == 1, n // 2 - lax.div(k, 2), n // 2 + lax.div(k, 2))


def kernel(
    points_hbm, scale_hbm, noise_hbm, residual_hbm, direction_hbm, out,
    points, scale, noise, residual, direction, send, jbuf, ibuf, jop, jdir, jacc, iop, idir, oown, own, probs, obuf, cpart, rpart, sums, csum, sums2, rsum,
    in_sem, send_sem, jsem, isem, osend, csem, rsem, ssend, ssem, ssem2,
):
    r, c = lax.axis_index("row"), lax.axis_index("col")

    def row_peer(d):
        return (lax.rem(r + d, ROWS), c)

    def col_peer(d):
        return (r, lax.rem(c + d + COLS, COLS))

    def shift(i):
        d = HALF + 1 - i
        return jnp.where(lax.rem(d, 2) == 1, d, -d)

    staged = ((points_hbm, points), (scale_hbm, scale), (noise_hbm, noise), (residual_hbm, residual), (direction_hbm, direction))
    for n, (src, dst) in enumerate(staged):
        pltpu.make_async_copy(src, dst, in_sem.at[n]).start()

    barrier = pltpu.get_barrier_semaphore()

    def greet(k, _):
        @pl.when(k < ROWS)
        def _row():
            pl.semaphore_signal(barrier, inc=1, device_id=row_peer(far_first(k, ROWS)), device_id_type=MESH)
        pl.semaphore_signal(barrier, inc=1, device_id=col_peer(shift(k)), device_id_type=MESH)
        return _

    lax.fori_loop(1, HALF + 1, greet, 0, unroll=True)

    for n, (src, dst) in enumerate(staged):
        pltpu.make_async_copy(src, dst, in_sem.at[n]).wait()
    dirs = direction[...]
    send[:F, :] = encode(points[...])
    send[F:, :] = dirs.astype(bf16)
    factor = jnp.broadcast_to(scale[...], (B, F)).T[:, :1] * (SQRT_LOG2E / CODE)

    pl.semaphore_wait(barrier, ROWS - 1 + HALF)

    def to_row(p):
        return pltpu.make_async_remote_copy(
            src_ref=send, dst_ref=jbuf.at[p], send_sem=send_sem, recv_sem=jsem.at[p],
            device_id=row_peer(ROWS - far_first(p, ROWS)), device_id_type=MESH)

    def to_col(i):
        return pltpu.make_async_remote_copy(
            src_ref=send, dst_ref=ibuf.at[i - 1], send_sem=send_sem, recv_sem=isem.at[i - 1],
            device_id=col_peer(-shift(i)), device_id_type=MESH)

    def push(k, _):
        @pl.when(k < ROWS)
        def _row():
            to_row(k).start()
        to_col(k).start()
        return _

    lax.fori_loop(1, HALF + 1, push, 0, unroll=True)

    def slot(n):
        return pl.ds(pl.multiple_of(n * B, B), B)

    def side_by_side(blocks):
        return jnp.concatenate(blocks, axis=1)

    def take_j(q, _):
        for n in range(GROUP):
            @pl.when(q * GROUP + n > 0)
            def _arrived():
                to_row(q * GROUP + n).wait_recv()
        part = lax.div(q, 2)
        place = pl.ds(pl.multiple_of(lax.rem(q, 2) * GROUP * B, GROUP * B), GROUP * B)
        blocks = [jbuf[q * GROUP + n] for n in range(GROUP)]
        jop[part, :, place] = j_operand(decode(side_by_side([m[:F] for m in blocks]), factor))
        jdir[part, :, place] = side_by_side([m[F:] for m in blocks])
        return _

    def take_i(g):
        for n in range(GROUP):
            to_col(g * GROUP + n + 1).wait_recv()
        weight = jnp.where(g == 0, 0.5, 1.0)
        blocks = [ibuf[g * GROUP + n] for n in range(GROUP)]
        iop[g] = i_operand(decode(side_by_side([m[:F] for m in blocks]), factor))
        first = (blocks[0][F:].astype(f32) * weight).astype(bf16)
        idir[g] = side_by_side([first] + [m[F:] for m in blocks[1:]])

    def tile(left, dirs_i, h, probs):
        for n in range(WIDTH // CHUNK):
            part = pl.ds(n * CHUNK, CHUNK)
            s = jnp.dot(left, jop[h, :, part], preferred_element_type=f32)
            probs[:, part] = jnp.exp2(s).astype(bf16)
        jacc[h] += jnp.dot(dirs_i, probs[...], preferred_element_type=f32)
        return lax.dot_general(jdir[h], probs[...], (((1,), (1,)), ((), ())), preferred_element_type=f32)

    def to_owner(n, g):
        i = g * GROUP + n
        return pltpu.make_async_remote_copy(
            src_ref=obuf.at[g, :, slot(n)], dst_ref=cpart.at[i], send_sem=osend, recv_sem=csem,
            device_id=col_peer(shift(i + 1)), device_id_type=MESH)

    def push_o(n, g):
        to_owner(n, g).start()
        return g

    def to_row_owner(p):
        d = far_first(p, ROWS)
        return pltpu.make_async_remote_copy(
            src_ref=jacc.at[lax.div(p, ROWS // 2), :, slot(lax.rem(p, ROWS // 2))], dst_ref=rpart.at[d - 1],
            send_sem=osend, recv_sem=rsem, device_id=row_peer(d), device_id_type=MESH)

    def push_j(p, _):
        to_row_owner(p).start()
        return _

    jbuf[0] = send[...]
    oown[...] = i_operand(decode(send[:F], factor))
    jacc[...] = jnp.zeros(jacc.shape, f32)
    obuf[...] = jnp.zeros(obuf.shape, f32)
    own[...] = jnp.zeros(own.shape, f32)

    def step_of(t, _):
        g, h = lax.rem(t, GROUPS), lax.div(t, GROUPS)

        @pl.when(g == 0)
        def _half():
            lax.fori_loop(2 * h, 2 * h + 2, take_j, 0)
            own[...] += 0.5 * tile(oown[...], send[F:] * bf16(0.5), h, probs.at[:B])

        @pl.when(h == 0)
        def _group():
            take_i(g)

        obuf[g] += tile(iop[g], idir[g], h, probs)

        @pl.when(t == GROUPS)
        def _half_weight():
            obuf[0, :, :B] = 0.5 * obuf[0, :, :B]

        @pl.when(h == 1)
        def _rows_done():
            lax.fori_loop(0, GROUP, push_o, g)

        @pl.when(g == GROUPS - 1)
        def _columns_done():
            lax.fori_loop(jnp.maximum(h * (ROWS // 2), 1), (h + 1) * (ROWS // 2), push_j, 0)
        return _

    lax.fori_loop(0, 2 * GROUPS, step_of, 0)

    res = residual[...]
    total = own[...] + jacc[0, :, :B] + noise[...] * dirs

    def whole(src, dst, s_sem, r_sem):
        return pltpu.make_async_remote_copy(
            src_ref=src, dst_ref=dst, send_sem=s_sem, recv_sem=r_sem,
            device_id=row_peer(1), device_id_type=MESH)

    whole(cpart, cpart, osend, csem).wait_recv()
    total += jnp.sum(cpart[...], axis=0)
    whole(rpart, rpart, osend, rsem).wait_recv()
    image = total + jnp.sum(rpart[...], axis=0)

    ahead = lax.broadcasted_iota(jnp.int32, (R, B), 1) - lax.broadcasted_iota(jnp.int32, (R, B), 0)
    local = jnp.zeros((R, B), f32)
    for n, prod in enumerate((res * res, res * image, dirs * image, image * image)):
        local = jnp.where(ahead == n * R, jnp.sum(prod, axis=1, keepdims=True), local)
    sums[...] = jnp.sum(local, axis=0, keepdims=True)

    def sum_to_col(d):
        return pltpu.make_async_remote_copy(
            src_ref=sums, dst_ref=csum.at[pl.ds(d - 1, 1)], send_sem=ssend, recv_sem=ssem,
            device_id=col_peer(d), device_id_type=MESH)

    def push_c(k, _):
        sum_to_col(far_first(k, COLS)).start()
        return _

    lax.fori_loop(1, COLS, push_c, 0, unroll=True)
    whole(csum, csum, ssend, ssem).wait_recv()
    sums2[...] = sums[...] + jnp.sum(csum[...], axis=0, keepdims=True)

    def sum_to_row(d):
        return pltpu.make_async_remote_copy(
            src_ref=sums2, dst_ref=rsum.at[pl.ds(d - 1, 1)], send_sem=ssend, recv_sem=ssem2,
            device_id=row_peer(d), device_id_type=MESH)

    def push_r(k, _):
        sum_to_row(far_first(k, ROWS)).start()
        return _

    lax.fori_loop(1, ROWS, push_r, 0, unroll=True)
    whole(rsum, rsum, ssend, ssem2).wait_recv()
    tot = sums2[...] + jnp.sum(rsum[...], axis=0, keepdims=True)
    rr, rq, dq, qq = (jnp.sum(jnp.where(ahead == n * R, tot, 0.0), axis=1, keepdims=True) for n in range(4))
    step = rr / dq
    nxt = rr - 2.0 * step * rq + step * (step * qq)
    out[:R, :] = image
    out[R:2 * R, :] = jnp.broadcast_to(step, (R, B))
    out[2 * R:, :] = jnp.broadcast_to(nxt / rr, (R, B))

    whole(jbuf.at[pl.ds(1, ROWS - 1)], jbuf.at[pl.ds(1, ROWS - 1)], send_sem, jsem.at[0]).wait_send()
    whole(ibuf, ibuf, send_sem, jsem.at[0]).wait_send()
    whole(cpart, cpart, osend, csem).wait_send()
    whole(rpart, rpart, osend, rsem).wait_send()
    whole(csum, csum, ssend, ssem).wait_send()
    whole(rsum, rsum, ssend, ssem2).wait_send()


def on_device(points, inv_scale, noise_var, residual, direction):
    vmem = pl.BlockSpec(memory_space=pltpu.VMEM)
    dma = pltpu.SemaphoreType.DMA
    found = pl.pallas_call(
        kernel,
        out_shape=pltpu.VMEM((3 * R, B), f32),
        in_specs=[pl.BlockSpec(memory_space=pltpu.HBM)] * 5,
        out_specs=vmem,
        scratch_shapes=[
            pltpu.VMEM((F, B), f32),
            pltpu.VMEM((1, F), f32),
            pltpu.VMEM((1, B), f32),
            pltpu.VMEM((R, B), f32),
            pltpu.VMEM((R, B), f32),
            pltpu.VMEM((MSG, B), bf16),
            pltpu.VMEM((ROWS, MSG, B), bf16),
            pltpu.VMEM((HALF, MSG, B), bf16),
            pltpu.VMEM((2, DEPTH, WIDTH), bf16),
            pltpu.VMEM((2, R, WIDTH), bf16),
            pltpu.VMEM((2, R, WIDTH), f32),
            pltpu.VMEM((GROUPS, GROUP * B, DEPTH), bf16),
            pltpu.VMEM((GROUPS, R, GROUP * B), bf16),
            pltpu.VMEM((B, DEPTH), bf16),
            pltpu.VMEM((R, B), f32),
            pltpu.VMEM((GROUP * B, WIDTH), bf16),
            pltpu.VMEM((GROUPS, R, GROUP * B), f32),
            pltpu.VMEM((HALF, R, B), f32),
            pltpu.VMEM((ROWS - 1, R, B), f32),
            pltpu.VMEM((1, B), f32),
            pltpu.VMEM((COLS - 1, B), f32),
            pltpu.VMEM((1, B), f32),
            pltpu.VMEM((ROWS - 1, B), f32),
            dma((5,)), dma, dma((ROWS,)), dma((HALF,)), dma, dma, dma, dma, dma, dma,
        ],
        compiler_params=pltpu.CompilerParams(
            collective_id=0, has_side_effects=True, vmem_limit_bytes=60 << 20),
    )(points, inv_scale.reshape(1, F), noise_var.reshape(1, B), residual, direction)
    image, step, ratio = found[:R], found[R:2 * R], found[2 * R:]
    residual_next = residual - step * image
    return residual_next, residual_next + ratio * direction


def solution(mesh):
    split_points = P(None, ("row", "col"))
    return jax.shard_map(
        on_device,
        mesh=mesh,
        in_specs=(split_points, P(), P(("row", "col")), split_points, split_points),
        out_specs=(split_points, split_points),
        check_vma=False,
    )
```

```python
import functools
import math

import jax
import jax.numpy as jnp
from jax import lax
from jax.experimental import pallas as pl
from jax.experimental.pallas import tpu as pltpu
from jax.sharding import PartitionSpec as P

MESH = pl.DeviceIdType.MESH
F = 64
R = 16
B = 128
ROWS, COLS = 16, 32
HALF = COLS // 2
MSG = F + R
DEPTH = 256
KEEP = 48
GROUP, GROUPS = 4, 4
WIDTH = ROWS * B // 2
CHUNK = 256
CODE = 250.0 / 6.0
BIAS = 125.0
SQRT_LOG2E = math.sqrt(math.log2(math.e))
bf16, f32 = jnp.bfloat16, jnp.float32


def encode(x):
    mag = jnp.exp2(jnp.abs(x) * CODE - BIAS)
    return jnp.where(x < 0, -mag, mag).astype(bf16)


def decode(code, factor):
    y = code.astype(f32)
    mag = (jnp.log2(jnp.abs(y)) + BIAS) * factor
    return jnp.where(y < 0, -mag, mag)


def split(a):
    hi = a.astype(bf16)
    hi32 = hi.astype(f32)
    mid = (a - hi32).astype(bf16)
    mid32 = mid.astype(f32)
    norm = -jnp.sum(hi32 * (0.5 * hi32 + mid32), axis=0, keepdims=True)
    n0 = norm.astype(bf16).astype(f32)
    n1 = (norm - n0).astype(bf16).astype(f32)
    n2 = norm - n0 - n1
    return hi, mid, (n0, n1, n2)


def aux_rows(norms, first):
    row = lax.broadcasted_iota(jnp.int32, (16, norms[0].shape[1]), 0)
    out = jnp.where((row >= 3 - first) & (row < 6 - first), 1.0, 0.0)
    for i, n in enumerate(norms):
        out = jnp.where(row == first + i, n, out)
    return out.astype(bf16)


def j_operand(a):
    hi, mid, norms = split(a)
    return jnp.concatenate([hi, mid, hi, mid[:KEEP], aux_rows(norms, 3)], axis=0)


def i_operand(a):
    hi, mid, norms = split(a)
    return jnp.concatenate([hi, hi, mid, mid[:KEEP], aux_rows(norms, 0)], axis=0).T


def far_first(k, n):
    return jnp.where(lax.rem(k, 2) == 1, n // 2 - lax.div(k, 2), n // 2 + lax.div(k, 2))


def kernel(
    points_hbm, scale_hbm, noise_hbm, residual_hbm, direction_hbm, out,
    points, scale, noise, residual, direction, send, jbuf, ibuf, jop, jdir, jacc, iop, idir, oown, own, probs, obuf, cpart, rpart, sums, csum, sums2, rsum,
    in_sem, send_sem, jsem, isem, osend, csem, rsem, ssend, ssem, ssem2,
):
    r, c = lax.axis_index("row"), lax.axis_index("col")

    def row_peer(d):
        return (lax.rem(r + d, ROWS), c)

    def col_peer(d):
        return (r, lax.rem(c + d + COLS, COLS))

    def shift(i):
        d = HALF + 1 - i
        return jnp.where(lax.rem(d, 2) == 1, d, -d)

    staged = ((points_hbm, points), (scale_hbm, scale), (noise_hbm, noise), (residual_hbm, residual), (direction_hbm, direction))
    for n, (src, dst) in enumerate(staged):
        pltpu.make_async_copy(src, dst, in_sem.at[n]).start()

    barrier = pltpu.get_barrier_semaphore()

    def greet(k, _):
        @pl.when(k < ROWS)
        def _row():
            pl.semaphore_signal(barrier, inc=1, device_id=row_peer(far_first(k, ROWS)), device_id_type=MESH)
        pl.semaphore_signal(barrier, inc=1, device_id=col_peer(shift(k)), device_id_type=MESH)
        return _

    lax.fori_loop(1, HALF + 1, greet, 0, unroll=True)

    for n, (src, dst) in enumerate(staged):
        pltpu.make_async_copy(src, dst, in_sem.at[n]).wait()
    dirs = direction[...]
    send[:F, :] = encode(points[...])
    send[F:, :] = dirs.astype(bf16)
    factor = jnp.broadcast_to(scale[...], (B, F)).T[:, :1] * (SQRT_LOG2E / CODE)

    pl.semaphore_wait(barrier, ROWS - 1 + HALF)

    def to_row(p):
        return pltpu.make_async_remote_copy(
            src_ref=send, dst_ref=jbuf.at[p], send_sem=send_sem, recv_sem=jsem.at[p],
            device_id=row_peer(ROWS - far_first(p, ROWS)), device_id_type=MESH)

    def to_col(i):
        return pltpu.make_async_remote_copy(
            src_ref=send, dst_ref=ibuf.at[i - 1], send_sem=send_sem, recv_sem=isem.at[i - 1],
            device_id=col_peer(-shift(i)), device_id_type=MESH)

    def push(k, _):
        @pl.when(k < ROWS)
        def _row():
            to_row(k).start()
        to_col(k).start()
        return _

    lax.fori_loop(1, HALF + 1, push, 0, unroll=True)

    def slot(n):
        return pl.ds(pl.multiple_of(n * B, B), B)

    def side_by_side(blocks):
        return jnp.concatenate(blocks, axis=1)

    def take_j(q, _):
        for n in range(GROUP):
            @pl.when(q * GROUP + n > 0)
            def _arrived():
                to_row(q * GROUP + n).wait_recv()
        part = lax.div(q, 2)
        place = pl.ds(pl.multiple_of(lax.rem(q, 2) * GROUP * B, GROUP * B), GROUP * B)
        blocks = [jbuf[q * GROUP + n] for n in range(GROUP)]
        jop[part, :, place] = j_operand(decode(side_by_side([m[:F] for m in blocks]), factor))
        jdir[part, :, place] = side_by_side([m[F:] for m in blocks])
        return _

    def take_i(g):
        for n in range(GROUP):
            to_col(g * GROUP + n + 1).wait_recv()
        weight = jnp.where(g == 0, 0.5, 1.0)
        blocks = [ibuf[g * GROUP + n] for n in range(GROUP)]
        iop[g] = i_operand(decode(side_by_side([m[:F] for m in blocks]), factor))
        first = (blocks[0][F:].astype(f32) * weight).astype(bf16)
        idir[g] = side_by_side([first] + [m[F:] for m in blocks[1:]])

    def tile(left, dirs_i, h, probs):
        for n in range(WIDTH // CHUNK):
            part = pl.ds(n * CHUNK, CHUNK)
            s = jnp.dot(left, jop[h, :, part], preferred_element_type=f32)
            probs[:, part] = jnp.exp2(s).astype(bf16)
        jacc[h] += jnp.dot(dirs_i, probs[...], preferred_element_type=f32)
        return lax.dot_general(jdir[h], probs[...], (((1,), (1,)), ((), ())), preferred_element_type=f32)

    def to_owner(n, g):
        i = g * GROUP + n
        return pltpu.make_async_remote_copy(
            src_ref=obuf.at[g, :, slot(n)], dst_ref=cpart.at[i], send_sem=osend, recv_sem=csem,
            device_id=col_peer(shift(i + 1)), device_id_type=MESH)

    def push_o(n, g):
        to_owner(n, g).start()
        return g

    def to_row_owner(p):
        d = far_first(p, ROWS)
        return pltpu.make_async_remote_copy(
            src_ref=jacc.at[lax.div(p, ROWS // 2), :, slot(lax.rem(p, ROWS // 2))], dst_ref=rpart.at[d - 1],
            send_sem=osend, recv_sem=rsem, device_id=row_peer(d), device_id_type=MESH)

    def push_j(p, _):
        to_row_owner(p).start()
        return _

    jbuf[0] = send[...]
    oown[...] = i_operand(decode(send[:F], factor))
    jacc[...] = jnp.zeros(jacc.shape, f32)
    obuf[...] = jnp.zeros(obuf.shape, f32)
    own[...] = jnp.zeros(own.shape, f32)

    def step_of(t, _):
        g, h = lax.rem(t, GROUPS), lax.div(t, GROUPS)

        @pl.when(g == 0)
        def _half():
            lax.fori_loop(2 * h, 2 * h + 2, take_j, 0)
            own[...] += 0.5 * tile(oown[...], send[F:] * bf16(0.5), h, probs.at[:B])

        @pl.when(h == 0)
        def _group():
            take_i(g)

        obuf[g] += tile(iop[g], idir[g], h, probs)

        @pl.when(t == GROUPS)
        def _half_weight():
            obuf[0, :, :B] = 0.5 * obuf[0, :, :B]

        @pl.when(h == 1)
        def _rows_done():
            lax.fori_loop(0, GROUP, push_o, g)

        @pl.when(g == GROUPS - 1)
        def _columns_done():
            lax.fori_loop(jnp.maximum(h * (ROWS // 2), 1), (h + 1) * (ROWS // 2), push_j, 0)
        return _

    lax.fori_loop(0, 2 * GROUPS, step_of, 0)

    res = residual[...]
    ahead = lax.broadcasted_iota(jnp.int32, (R, B), 1) - lax.broadcasted_iota(jnp.int32, (R, B), 0)
    local = jnp.where(ahead == 0, jnp.sum(res * res, axis=1, keepdims=True), 0.0)
    total = own[...] + jacc[0, :, :B] + noise[...] * dirs

    def whole(src, dst, s_sem, r_sem):
        return pltpu.make_async_remote_copy(
            src_ref=src, dst_ref=dst, send_sem=s_sem, recv_sem=r_sem,
            device_id=row_peer(1), device_id_type=MESH)

    whole(cpart, cpart, osend, csem).wait_recv()
    total += jnp.sum(cpart[...], axis=0)
    whole(rpart, rpart, osend, rsem).wait_recv()
    image = total + jnp.sum(rpart[...], axis=0)

    for n, prod in enumerate((res * image, dirs * image, image * image), 1):
        local = jnp.where(ahead == n * R, jnp.sum(prod, axis=1, keepdims=True), local)
    sums[...] = jnp.sum(local, axis=0, keepdims=True)

    def sum_to_col(d):
        return pltpu.make_async_remote_copy(
            src_ref=sums, dst_ref=csum.at[pl.ds(d - 1, 1)], send_sem=ssend, recv_sem=ssem,
            device_id=col_peer(d), device_id_type=MESH)

    def push_c(k, _):
        sum_to_col(far_first(k, COLS)).start()
        return _

    lax.fori_loop(1, COLS, push_c, 0, unroll=True)
    whole(csum, csum, ssend, ssem).wait_recv()
    sums2[...] = sums[...] + jnp.sum(csum[...], axis=0, keepdims=True)

    def sum_to_row(d):
        return pltpu.make_async_remote_copy(
            src_ref=sums2, dst_ref=rsum.at[pl.ds(d - 1, 1)], send_sem=ssend, recv_sem=ssem2,
            device_id=row_peer(d), device_id_type=MESH)

    def push_r(k, _):
        sum_to_row(far_first(k, ROWS)).start()
        return _

    lax.fori_loop(1, ROWS, push_r, 0, unroll=True)
    whole(rsum, rsum, ssend, ssem2).wait_recv()
    tot = sums2[...] + jnp.sum(rsum[...], axis=0, keepdims=True)
    rr, rq, dq, qq = (jnp.sum(jnp.where(ahead == n * R, tot, 0.0), axis=1, keepdims=True) for n in range(4))
    step = rr / dq
    nxt = rr - 2.0 * step * rq + step * (step * qq)
    out[:R, :] = image
    out[R:2 * R, :] = jnp.broadcast_to(step, (R, B))
    out[2 * R:, :] = jnp.broadcast_to(nxt / rr, (R, B))

    whole(jbuf.at[pl.ds(1, ROWS - 1)], jbuf.at[pl.ds(1, ROWS - 1)], send_sem, jsem.at[0]).wait_send()
    whole(ibuf, ibuf, send_sem, jsem.at[0]).wait_send()
    whole(cpart, cpart, osend, csem).wait_send()
    whole(rpart, rpart, osend, rsem).wait_send()
    whole(csum, csum, ssend, ssem).wait_send()
    whole(rsum, rsum, ssend, ssem2).wait_send()


def on_device(points, inv_scale, noise_var, residual, direction):
    vmem = pl.BlockSpec(memory_space=pltpu.VMEM)
    dma = pltpu.SemaphoreType.DMA
    found = pl.pallas_call(
        kernel,
        out_shape=pltpu.VMEM((3 * R, B), f32),
        in_specs=[pl.BlockSpec(memory_space=pltpu.HBM)] * 5,
        out_specs=vmem,
        scratch_shapes=[
            pltpu.VMEM((F, B), f32),
            pltpu.VMEM((1, F), f32),
            pltpu.VMEM((1, B), f32),
            pltpu.VMEM((R, B), f32),
            pltpu.VMEM((R, B), f32),
            pltpu.VMEM((MSG, B), bf16),
            pltpu.VMEM((ROWS, MSG, B), bf16),
            pltpu.VMEM((HALF, MSG, B), bf16),
            pltpu.VMEM((2, DEPTH, WIDTH), bf16),
            pltpu.VMEM((2, R, WIDTH), bf16),
            pltpu.VMEM((2, R, WIDTH), f32),
            pltpu.VMEM((GROUPS, GROUP * B, DEPTH), bf16),
            pltpu.VMEM((GROUPS, R, GROUP * B), bf16),
            pltpu.VMEM((B, DEPTH), bf16),
            pltpu.VMEM((R, B), f32),
            pltpu.VMEM((GROUP * B, WIDTH), bf16),
            pltpu.VMEM((GROUPS, R, GROUP * B), f32),
            pltpu.VMEM((HALF, R, B), f32),
            pltpu.VMEM((ROWS - 1, R, B), f32),
            pltpu.VMEM((1, B), f32),
            pltpu.VMEM((COLS - 1, B), f32),
            pltpu.VMEM((1, B), f32),
            pltpu.VMEM((ROWS - 1, B), f32),
            dma((5,)), dma, dma((ROWS,)), dma((HALF,)), dma, dma, dma, dma, dma, dma,
        ],
        compiler_params=pltpu.CompilerParams(
            collective_id=0, has_side_effects=True, vmem_limit_bytes=60 << 20),
    )(points, inv_scale.reshape(1, F), noise_var.reshape(1, B), residual, direction)
    image, step, ratio = found[:R], found[R:2 * R], found[2 * R:]
    residual_next = residual - step * image
    return residual_next, residual_next + ratio * direction


def solution(mesh):
    split_points = P(None, ("row", "col"))
    return jax.shard_map(
        on_device,
        mesh=mesh,
        in_specs=(split_points, P(), P(("row", "col")), split_points, split_points),
        out_specs=(split_points, split_points),
        check_vma=False,
    )
```

```python
import functools
import math

import jax
import jax.numpy as jnp
from jax import lax
from jax.experimental import pallas as pl
from jax.experimental.pallas import tpu as pltpu
from jax.sharding import PartitionSpec as P

MESH = pl.DeviceIdType.MESH
F = 64
R = 16
B = 128
ROWS, COLS = 16, 32
HALF = COLS // 2
MSG = F + R
DEPTH = 256
KEEP = 48
GROUP, GROUPS = 4, 4
WIDTH = ROWS * B // 2
CHUNK = 512
CODE = 250.0 / 6.0
BIAS = 125.0
SQRT_LOG2E = math.sqrt(math.log2(math.e))
bf16, f32 = jnp.bfloat16, jnp.float32


def encode(x):
    mag = jnp.exp2(jnp.abs(x) * CODE - BIAS)
    return jnp.where(x < 0, -mag, mag).astype(bf16)


def decode(code, factor):
    y = code.astype(f32)
    mag = (jnp.log2(jnp.abs(y)) + BIAS) * factor
    return jnp.where(y < 0, -mag, mag)


def split(a):
    hi = a.astype(bf16)
    hi32 = hi.astype(f32)
    mid = (a - hi32).astype(bf16)
    mid32 = mid.astype(f32)
    norm = -jnp.sum(hi32 * (0.5 * hi32 + mid32), axis=0, keepdims=True)
    n0 = norm.astype(bf16).astype(f32)
    n1 = (norm - n0).astype(bf16).astype(f32)
    n2 = norm - n0 - n1
    return hi, mid, (n0, n1, n2)


def aux_rows(norms, first):
    row = lax.broadcasted_iota(jnp.int32, (16, norms[0].shape[1]), 0)
    out = jnp.where((row >= 3 - first) & (row < 6 - first), 1.0, 0.0)
    for i, n in enumerate(norms):
        out = jnp.where(row == first + i, n, out)
    return out.astype(bf16)


def j_operand(a):
    hi, mid, norms = split(a)
    return jnp.concatenate([hi, mid, hi, mid[:KEEP], aux_rows(norms, 3)], axis=0)


def i_operand(a):
    hi, mid, norms = split(a)
    return jnp.concatenate([hi, hi, mid, mid[:KEEP], aux_rows(norms, 0)], axis=0).T


def far_first(k, n):
    return jnp.where(lax.rem(k, 2) == 1, n // 2 - lax.div(k, 2), n // 2 + lax.div(k, 2))


def kernel(
    points_hbm, scale_hbm, noise_hbm, residual_hbm, direction_hbm, out,
    points, scale, noise, residual, direction, send, jbuf, ibuf, jop, jdir, jacc, iop, idir, oown, own, probs, obuf, cpart, rpart, sums, csum, sums2, rsum,
    in_sem, send_sem, jsem, isem, osend, csem, rsem, ssend, ssem, ssem2,
):
    r, c = lax.axis_index("row"), lax.axis_index("col")

    def row_peer(d):
        return (lax.rem(r + d, ROWS), c)

    def col_peer(d):
        return (r, lax.rem(c + d + COLS, COLS))

    def shift(i):
        d = HALF + 1 - i
        return jnp.where(lax.rem(d, 2) == 1, d, -d)

    barrier = pltpu.get_barrier_semaphore()

    def greet(k, _):
        @pl.when(k < ROWS)
        def _row():
            pl.semaphore_signal(barrier, inc=1, device_id=row_peer(far_first(k, ROWS)), device_id_type=MESH)
        pl.semaphore_signal(barrier, inc=1, device_id=col_peer(shift(k)), device_id_type=MESH)
        return _

    lax.fori_loop(1, HALF + 1, greet, 0, unroll=True)

    staged = ((points_hbm, points), (scale_hbm, scale), (noise_hbm, noise), (residual_hbm, residual), (direction_hbm, direction))
    for n, (src, dst) in enumerate(staged):
        pltpu.make_async_copy(src, dst, in_sem.at[n]).start()

    for n, (src, dst) in enumerate(staged):
        pltpu.make_async_copy(src, dst, in_sem.at[n]).wait()
    dirs = direction[...]
    send[:F, :] = encode(points[...])
    send[F:, :] = dirs.astype(bf16)
    factor = jnp.broadcast_to(scale[...], (B, F)).T[:, :1] * (SQRT_LOG2E / CODE)

    pl.semaphore_wait(barrier, ROWS - 1 + HALF)

    def to_row(p):
        return pltpu.make_async_remote_copy(
            src_ref=send, dst_ref=jbuf.at[p], send_sem=send_sem, recv_sem=jsem.at[p],
            device_id=row_peer(ROWS - far_first(p, ROWS)), device_id_type=MESH)

    def to_col(i):
        return pltpu.make_async_remote_copy(
            src_ref=send, dst_ref=ibuf.at[i - 1], send_sem=send_sem, recv_sem=isem.at[i - 1],
            device_id=col_peer(-shift(i)), device_id_type=MESH)

    def push(k, _):
        @pl.when(k < ROWS)
        def _row():
            to_row(k).start()
        to_col(k).start()
        return _

    lax.fori_loop(1, HALF + 1, push, 0, unroll=True)

    def slot(n):
        return pl.ds(pl.multiple_of(n * B, B), B)

    def side_by_side(blocks):
        return jnp.concatenate(blocks, axis=1)

    def take_j(q, _):
        for n in range(GROUP):
            @pl.when(q * GROUP + n > 0)
            def _arrived():
                to_row(q * GROUP + n).wait_recv()
        part = lax.div(q, 2)
        place = pl.ds(pl.multiple_of(lax.rem(q, 2) * GROUP * B, GROUP * B), GROUP * B)
        blocks = [jbuf[q * GROUP + n] for n in range(GROUP)]
        jop[part, :, place] = j_operand(decode(side_by_side([m[:F] for m in blocks]), factor))
        jdir[part, :, place] = side_by_side([m[F:] for m in blocks])
        return _

    def take_i(g):
        for n in range(GROUP):
            to_col(g * GROUP + n + 1).wait_recv()
        weight = jnp.where(g == 0, 0.5, 1.0)
        blocks = [ibuf[g * GROUP + n] for n in range(GROUP)]
        iop[g] = i_operand(decode(side_by_side([m[:F] for m in blocks]), factor))
        first = (blocks[0][F:].astype(f32) * weight).astype(bf16)
        idir[g] = side_by_side([first] + [m[F:] for m in blocks[1:]])

    def tile(left, dirs_i, h, probs):
        for n in range(WIDTH // CHUNK):
            part = pl.ds(n * CHUNK, CHUNK)
            s = jnp.dot(left, jop[h, :, part], preferred_element_type=f32)
            probs[:, part] = jnp.exp2(s).astype(bf16)
        jacc[h] += jnp.dot(dirs_i, probs[...], preferred_element_type=f32)
        return lax.dot_general(jdir[h], probs[...], (((1,), (1,)), ((), ())), preferred_element_type=f32)

    def to_owner(n, g):
        i = g * GROUP + n
        return pltpu.make_async_remote_copy(
            src_ref=obuf.at[g, :, slot(n)], dst_ref=cpart.at[i], send_sem=osend, recv_sem=csem,
            device_id=col_peer(shift(i + 1)), device_id_type=MESH)

    def push_o(n, g):
        to_owner(n, g).start()
        return g

    def to_row_owner(p):
        d = far_first(p, ROWS)
        return pltpu.make_async_remote_copy(
            src_ref=jacc.at[lax.div(p, ROWS // 2), :, slot(lax.rem(p, ROWS // 2))], dst_ref=rpart.at[d - 1],
            send_sem=osend, recv_sem=rsem, device_id=row_peer(d), device_id_type=MESH)

    def push_j(p, _):
        to_row_owner(p).start()
        return _

    jbuf[0] = send[...]
    oown[...] = i_operand(decode(send[:F], factor))
    jacc[...] = jnp.zeros(jacc.shape, f32)
    own[...] = jnp.zeros(own.shape, f32)

    def half_of_j(h):
        lax.fori_loop(2 * h, 2 * h + 2, take_j, 0)
        own[...] += 0.5 * tile(oown[...], send[F:] * bf16(0.5), h, probs.at[:B])

    def push_half(h):
        for p in range(max(h * (ROWS // 2), 1), (h + 1) * (ROWS // 2)):
            push_j(p, 0)

    def one_group(g, _):
        take_i(g)
        obuf[g] = tile(iop[g], idir[g], 0, probs.at[:GROUP * B])
        return _

    def two_groups(u, _):
        g = 2 * u
        left = jnp.concatenate([iop[g], iop[g + 1]], axis=0)
        out = tile(left, side_by_side([idir[g], idir[g + 1]]), 1, probs)
        obuf[g] += out[:, :GROUP * B]
        obuf[g + 1] += out[:, GROUP * B:]

        @pl.when(u == 0)
        def _half_weight():
            obuf[0, :, :B] = 0.5 * obuf[0, :, :B]

        for n in range(GROUP):
            push_o(n, g)
        for n in range(GROUP):
            push_o(n, g + 1)
        return _

    half_of_j(0)
    lax.fori_loop(0, GROUPS, one_group, 0)
    push_half(0)
    half_of_j(1)
    lax.fori_loop(0, GROUPS // 2, two_groups, 0)
    push_half(1)

    res = residual[...]
    total = own[...] + jacc[0, :, :B] + noise[...] * dirs

    def whole(src, dst, s_sem, r_sem):
        return pltpu.make_async_remote_copy(
            src_ref=src, dst_ref=dst, send_sem=s_sem, recv_sem=r_sem,
            device_id=row_peer(1), device_id_type=MESH)

    whole(cpart, cpart, osend, csem).wait_recv()
    total += jnp.sum(cpart[...], axis=0)
    whole(rpart, rpart, osend, rsem).wait_recv()
    image = total + jnp.sum(rpart[...], axis=0)

    ahead = lax.broadcasted_iota(jnp.int32, (R, B), 1) - lax.broadcasted_iota(jnp.int32, (R, B), 0)
    local = jnp.zeros((R, B), f32)
    for n, prod in enumerate((res * res, res * image, dirs * image, image * image)):
        local = jnp.where(ahead == n * R, jnp.sum(prod, axis=1, keepdims=True), local)
    sums[...] = jnp.sum(local, axis=0, keepdims=True)

    def sum_to_col(d):
        return pltpu.make_async_remote_copy(
            src_ref=sums, dst_ref=csum.at[pl.ds(d - 1, 1)], send_sem=ssend, recv_sem=ssem,
            device_id=col_peer(d), device_id_type=MESH)

    def push_c(k, _):
        sum_to_col(far_first(k, COLS)).start()
        return _

    lax.fori_loop(1, COLS, push_c, 0, unroll=True)
    whole(csum, csum, ssend, ssem).wait_recv()
    sums2[...] = sums[...] + jnp.sum(csum[...], axis=0, keepdims=True)

    def sum_to_row(d):
        return pltpu.make_async_remote_copy(
            src_ref=sums2, dst_ref=rsum.at[pl.ds(d - 1, 1)], send_sem=ssend, recv_sem=ssem2,
            device_id=row_peer(d), device_id_type=MESH)

    def push_r(k, _):
        sum_to_row(far_first(k, ROWS)).start()
        return _

    lax.fori_loop(1, ROWS, push_r, 0, unroll=True)
    whole(rsum, rsum, ssend, ssem2).wait_recv()
    tot = sums2[...] + jnp.sum(rsum[...], axis=0, keepdims=True)
    rr, rq, dq, qq = (jnp.sum(jnp.where(ahead == n * R, tot, 0.0), axis=1, keepdims=True) for n in range(4))
    step = rr / dq
    nxt = rr - 2.0 * step * rq + step * (step * qq)
    out[:R, :] = image
    out[R:2 * R, :] = jnp.broadcast_to(step, (R, B))
    out[2 * R:, :] = jnp.broadcast_to(nxt / rr, (R, B))

    whole(jbuf.at[pl.ds(1, ROWS - 1)], jbuf.at[pl.ds(1, ROWS - 1)], send_sem, jsem.at[0]).wait_send()
    whole(ibuf, ibuf, send_sem, jsem.at[0]).wait_send()
    whole(cpart, cpart, osend, csem).wait_send()
    whole(rpart, rpart, osend, rsem).wait_send()
    whole(csum, csum, ssend, ssem).wait_send()
    whole(rsum, rsum, ssend, ssem2).wait_send()


def on_device(points, inv_scale, noise_var, residual, direction):
    vmem = pl.BlockSpec(memory_space=pltpu.VMEM)
    dma = pltpu.SemaphoreType.DMA
    found = pl.pallas_call(
        kernel,
        out_shape=pltpu.VMEM((3 * R, B), f32),
        in_specs=[pl.BlockSpec(memory_space=pltpu.HBM)] * 5,
        out_specs=vmem,
        scratch_shapes=[
            pltpu.VMEM((F, B), f32),
            pltpu.VMEM((1, F), f32),
            pltpu.VMEM((1, B), f32),
            pltpu.VMEM((R, B), f32),
            pltpu.VMEM((R, B), f32),
            pltpu.VMEM((MSG, B), bf16),
            pltpu.VMEM((ROWS, MSG, B), bf16),
            pltpu.VMEM((HALF, MSG, B), bf16),
            pltpu.VMEM((2, DEPTH, WIDTH), bf16),
            pltpu.VMEM((2, R, WIDTH), bf16),
            pltpu.VMEM((2, R, WIDTH), f32),
            pltpu.VMEM((GROUPS, GROUP * B, DEPTH), bf16),
            pltpu.VMEM((GROUPS, R, GROUP * B), bf16),
            pltpu.VMEM((B, DEPTH), bf16),
            pltpu.VMEM((R, B), f32),
            pltpu.VMEM((2 * GROUP * B, WIDTH), bf16),
            pltpu.VMEM((GROUPS, R, GROUP * B), f32),
            pltpu.VMEM((HALF, R, B), f32),
            pltpu.VMEM((ROWS - 1, R, B), f32),
            pltpu.VMEM((1, B), f32),
            pltpu.VMEM((COLS - 1, B), f32),
            pltpu.VMEM((1, B), f32),
            pltpu.VMEM((ROWS - 1, B), f32),
            dma((5,)), dma, dma((ROWS,)), dma((HALF,)), dma, dma, dma, dma, dma, dma,
        ],
        compiler_params=pltpu.CompilerParams(
            collective_id=0, has_side_effects=True, vmem_limit_bytes=60 << 20),
    )(points, inv_scale.reshape(1, F), noise_var.reshape(1, B), residual, direction)
    image, step, ratio = found[:R], found[R:2 * R], found[2 * R:]
    residual_next = residual - step * image
    return residual_next, residual_next + ratio * direction


def solution(mesh):
    split_points = P(None, ("row", "col"))
    return jax.shard_map(
        on_device,
        mesh=mesh,
        in_specs=(split_points, P(), P(("row", "col")), split_points, split_points),
        out_specs=(split_points, split_points),
        check_vma=False,
    )
```
